128 devices in a mesh: dp: 16 (over x_hi, z, core), owner: 8 (over y, x_lo).
Axes of the slice: x: 4 (x_hi: 2, x_lo: 2; x = x_hi * 2 + x_lo), y: 4, z: 4, core: 2. Of those that a mesh axis runs over, the one named last changes fastest.
Arguments:
- inputs: bfloat16 [8192, 6144], P('dp'), may hold values from -6 to 6
- out_grads: bfloat16 [8192, 6144], P('dp'), may hold values from -6 to 6
- kernel_grad: bfloat16 [6144, 6144], P('dp', 'owner'), may hold values from -6 to 6
- basis_in: bfloat16 [6144, 6144], P(('dp', 'owner')), may hold values from -0.078125 to 0.078125
- basis_out: bfloat16 [6144, 768], P('owner'), may hold values from -0.21875 to 0.21875
- eigen_in: float32 [6144], P('dp'), may hold values from 0.3 to 3
- eigen_out: float32 [6144], P('owner'), may hold values from 0.3 to 3
- old_in_factor: float32 [6144, 6144], P('dp', 'owner'), may hold values from -0.4 to 2.4, as said below
- old_out_factor: float32 [6144, 768], P(('owner', 'dp')), may hold values from -0.4 to 2.4, as said below
Outputs:
- precond: bfloat16 [6144, 6144], P(None, 'owner')
- in_factor: float32 [6144, 6144], P('dp', 'owner')
- out_factor: float32 [6144, 768], P(('owner', 'dp'))
The draws below stay inside these ranges and needn't reach their ends.
Inputs may be any that keep to these rules, and one draw needn't show every extreme that they name: `old_in_factor`: Symmetric, with a positive diagonal. `old_out_factor`: each block is symmetric, with a positive diagonal.
All inputs are finite; a program needn't handle non-finite values.
Results may differ from the reference program's by a relative error of at most 0.015.
Values may be sent and summed in bfloat16 or wider, within the bound.
A program may use at most 128 MiB of HBM per device.

```python
import math
import jax
import jax.numpy as jnp
from jax import lax

D = 6144
TOKENS = 8192
OUT_BLOCK = 768
N_DP = 16


def symmetric_factor(key, count, width):
    noise_key, diag_key = jax.random.split(key)
    noise = jax.random.truncated_normal(noise_key, -4.0, 4.0, (count, width, width), jnp.float32) * 0.05
    noise = noise + jnp.swapaxes(noise, 1, 2)
    diag_values = jnp.exp(jax.random.uniform(diag_key, (count, width, 1), jnp.float32, jnp.log(0.5), jnp.log(2.0)))
    rows = lax.broadcasted_iota(jnp.int32, (count, width, width), 1)
    cols = lax.broadcasted_iota(jnp.int32, (count, width, width), 2)
    return noise + jnp.where(rows == cols, diag_values, 0.0)


def draw_old_in_factor(key, part):
    key = jax.random.fold_in(key, 11)
    return symmetric_factor(key, 1, D).reshape(D, D)


def draw_old_out_factor(key, part):
    key = jax.random.fold_in(key, 23)
    return symmetric_factor(key, D // OUT_BLOCK, OUT_BLOCK).reshape(D, OUT_BLOCK)


def spiked(values, own_key, source, target, parts, factor):
    owner, partner = [(jnp.arange(values.shape[axis_at]) // (values.shape[axis_at] // parts)).reshape([-1 if axis == axis_at else 1 for axis in range(values.ndim)]) for axis_at in (source, target)]
    chosen = jax.random.permutation(own_key, parts)[partner]
    strong = (owner == chosen) | (owner == (partner + parts // 2) % parts)
    return jnp.where(strong, factor * values, values)


def levels(key, dims, cuts, least, largest):
    def one(dim, parts):
        steps = jax.random.uniform(jax.random.fold_in(jax.random.fold_in(key, 6), dim), (parts,), jnp.float32, least / len(cuts), largest / len(cuts))
        return jnp.repeat(jnp.exp(steps), dims[dim] // parts).reshape((-1,) + (1,) * (len(dims) - dim - 1))

    factor_of = one(*cuts[0])
    for cut in cuts[1:]:
        factor_of = factor_of * one(*cut)
    return factor_of


def normal_values(key, dims, spread, limit, pieces=(), kind=jnp.bfloat16):
    loudness = levels(key, dims, pieces, -0.22, 0.18) if pieces else 1.0
    values = jax.random.normal(key, dims, jnp.float32) * spread * loudness
    return jnp.minimum(jnp.maximum(values, -limit), limit).astype(kind)


def bell_draw_with(rng, shape, scale, most, cuts, heavy, held_as=jnp.bfloat16):
    entries = scale * jax.random.normal(rng, shape, jnp.float32)
    if cuts:
        entries = entries * levels(rng, shape, cuts, -0.22, 0.18)
    return jnp.clip(spiked(entries, jax.random.fold_in(rng, 3), *heavy), -most, most).astype(held_as)


def setup_inputs(seed: int = 0) -> dict:
    streams_of = jax.random.split(jax.random.key(seed), 10)
    return {
        "inputs": bell_draw_with(streams_of[0], (TOKENS, D), 1.0, 6.0, ((0, 16),), (0, 1, 16, 2.0)),
        "out_grads": bell_draw_with(streams_of[1], (TOKENS, D), 1.0, 6.0, ((0, 16),), (0, 1, 16, 2.0)),
        "kernel_grad": normal_values(streams_of[2], (D, D), 1.0, 6.0, ((0, 16), (1, 8))),
        "basis_in": normal_values(streams_of[3], (D, D), D ** -0.5, 0.078125, ((0, 128),)),
        "basis_out": normal_values(streams_of[4], (D, OUT_BLOCK), OUT_BLOCK ** -0.5, 0.21875, ((0, 8),)),
        "eigen_in": jnp.clip(jnp.exp(math.log(3.0) - 2.3025851 * jax.random.uniform(streams_of[5], (D,), jnp.float32) ** levels(streams_of[5], (D,), ((0, 16),), -0.2, 0.2)), 0.3, 3.0),
        "eigen_out": jnp.clip(jnp.exp(math.log(3.0) - 2.3025851 * jax.random.uniform(streams_of[6], (D,), jnp.float32) ** levels(streams_of[6], (D,), ((0, 8),), -0.2, 0.2)), 0.3, 3.0),
        "old_in_factor": draw_old_in_factor(jax.random.fold_in(streams_of[9], 71), 0),
        "old_out_factor": draw_old_out_factor(jax.random.fold_in(streams_of[9], 71), 0),
    }


damping = 0.3
factor_decay = 0.9


def grouped_gram(left, right, groups):
    left_groups = left.reshape(groups, -1, left.shape[1])
    right_groups = right.reshape(groups, -1, right.shape[1])

    def step(total, pair):
        part = jnp.dot(pair[0].T, pair[1], preferred_element_type=jnp.float32)
        rounded = lax.optimization_barrier(part.astype(jnp.bfloat16))
        return total + rounded.astype(jnp.float32), None

    start = jnp.zeros((left.shape[1], right.shape[1]), jnp.float32)
    total, unused = lax.scan(step, start, (left_groups, right_groups))
    return total


def reference(inputs, out_grads, kernel_grad, basis_in, basis_out, eigen_in, eigen_out, old_in_factor, old_out_factor):
    blocks = D // OUT_BLOCK
    in_cov = grouped_gram(inputs, inputs, N_DP)
    in_factor = factor_decay * old_in_factor + (1.0 - factor_decay) * in_cov / TOKENS
    out_parts = []
    turned_parts = []
    for block in range(blocks):
        lower = block * OUT_BLOCK
        upper = lower + OUT_BLOCK
        grads_block = out_grads[:, lower:upper]
        out_parts.append(grouped_gram(grads_block, grads_block, N_DP))
        turned_parts.append(jnp.dot(kernel_grad[:, lower:upper], basis_out[lower:upper, :], preferred_element_type=jnp.float32).astype(jnp.bfloat16))
    out_cov = jnp.concatenate(out_parts, 0)
    out_factor = factor_decay * old_out_factor + (1.0 - factor_decay) * out_cov / TOKENS
    turned = jnp.concatenate(turned_parts, 1)
    rotated = grouped_gram(basis_in, turned, N_DP)
    scaled = (rotated / (eigen_in[:, None] * eigen_out[None, :] + damping)).astype(jnp.bfloat16)
    restored = jnp.dot(basis_in, scaled, preferred_element_type=jnp.float32).astype(jnp.bfloat16)
    final_parts = []
    for block in range(blocks):
        lower = block * OUT_BLOCK
        upper = lower + OUT_BLOCK
        final_parts.append(jnp.dot(restored[:, lower:upper], basis_out[lower:upper, :].T, preferred_element_type=jnp.float32).astype(jnp.bfloat16))
    precond = jnp.concatenate(final_parts, 1)
    return precond, in_factor, out_factor
```

```python
import functools

import jax
import jax.numpy as jnp
from jax import lax
from jax.experimental import pallas as pl
from jax.experimental.pallas import tpu as pltpu
from jax.sharding import PartitionSpec as P

damping = 0.3
factor_decay = 0.9
MESH = pl.DeviceIdType.MESH
CHUNKS = 2
MESSAGES = 160
F32 = jnp.float32
BF16 = jnp.bfloat16


def dot_rows(left, right):
    return lax.dot_general(left, right, (((0,), (0,)), ((), ())), preferred_element_type=F32)


def dot(left, right):
    return jnp.dot(left, right, preferred_element_type=F32)


class Message:
    def __init__(self, pool, source, target, to):
        number = pool[2]
        pool[2] += 1
        self.copy = pltpu.make_async_remote_copy(
            src_ref=source,
            dst_ref=target,
            send_sem=pool[0].at[number],
            recv_sem=pool[1].at[number],
            device_id=to,
            device_id_type=MESH,
        )

    def start(self):
        self.copy.start()
        return self

    def arrived(self):
        self.copy.wait_recv()

    def sent(self):
        self.copy.wait_send()


class Gather:
    def __init__(self, pool, region, place, plus, minus):
        self.region, self.place, self.plus, self.minus, self.pool = region, place, plus, minus, pool
        self.own = {}
        self.passed = []

    def message(self, shard, half, to):
        piece = self.region(shard, half)
        return Message(self.pool, piece, piece, to).start()

    def start(self, half):
        order = (("plus", self.plus), ("minus", self.minus))
        for name, to in order if half == 0 else order[::-1]:
            self.own[name, half] = self.message(self.place, half, to)

    def forward(self):
        below, above = lax.rem(self.place + 3, 4), lax.rem(self.place + 1, 4)
        self.own["plus", 0].arrived()
        self.passed.append(self.message(below, 0, self.plus))
        self.own["minus", 1].arrived()
        self.passed.append(self.message(above, 1, self.minus))

    def near(self):
        self.own["minus", 0].arrived()
        self.own["plus", 1].arrived()

    def far(self):
        for message in self.passed:
            message.arrived()

    def sent(self):
        for message in list(self.own.values()) + self.passed:
            message.sent()


class Scatter:
    def __init__(self, pool, mine, transit, slots, place, plus, minus):
        self.pool, self.mine, self.transit, self.slots = pool, mine, transit, slots
        self.plus, self.minus = plus, minus
        self.here = place
        self.above, self.below, self.far = (lax.rem(place + step, 4) for step in (1, 3, 2))
        self.messages = []

    def send(self, source, target, to):
        message = Message(self.pool, source, target, to).start()
        self.messages.append(message)
        return message

    def start_far(self):
        self.up = self.send(self.mine(self.far, 0), self.transit(0), self.plus)
        self.down = self.send(self.mine(self.far, 1), self.transit(1), self.minus)

    def start_near(self):
        self.direct_up = self.send(self.mine(self.above, 1), self.slots(0), self.plus)
        self.direct_down = self.send(self.mine(self.below, 0), self.slots(1), self.minus)

    def forward(self):
        self.up.arrived()
        piece = self.mine(self.above, 0)
        piece[...] = (piece[...].astype(F32) + self.transit(0)[...].astype(F32)).astype(BF16)
        self.sum_up = self.send(piece, self.slots(2), self.plus)
        self.down.arrived()
        piece = self.mine(self.below, 1)
        piece[...] = (piece[...].astype(F32) + self.transit(1)[...].astype(F32)).astype(BF16)
        self.sum_down = self.send(piece, self.slots(3), self.minus)

    def arrived(self, half):
        if half == 0:
            self.direct_down.arrived()
            self.sum_up.arrived()
        else:
            self.direct_up.arrived()
            self.sum_down.arrived()

    def total(self, half):
        one, two = (1, 2) if half == 0 else (0, 3)
        return (
            self.mine(self.here, half)[...].astype(F32)
            + self.slots(one)[...].astype(F32)
            + self.slots(two)[...].astype(F32)
        )

    def sent(self):
        for message in self.messages:
            message.sent()


def kernel(
    inputs,
    grads,
    kernel_grad,
    basis_in,
    basis_out,
    eigen_in,
    eigen_out,
    gathered,
    in_cov,
    out_cov,
    basis,
    turned,
    part,
    part_transit,
    part_slots,
    scaled,
    eigen_rows,
    eigen_columns,
    away,
    away_in,
    home,
    home_sum,
    home_transit,
    home_slots,
    tokens,
    token_columns,
    grad_columns,
    grad_part,
    cov,
    cov_transit,
    cov_slots,
    cov_across,
    grad_tile,
    basis_out_tile,
    local,
    send,
    receive,
):
    pool = [send, receive, 0]
    rows = kernel_grad.shape[0]
    width = kernel_grad.shape[1]
    strip = basis_in.shape[0]
    out_rows = out_cov.shape[0]
    narrow = width // 4
    dp, owner = lax.axis_index("dp"), lax.axis_index("owner")
    xh, z, c = dp // 8, lax.rem(dp // 2, 4), lax.rem(dp, 2)
    y, xl = owner // 2, lax.rem(owner, 2)
    x = xh * 2 + xl

    def device(x, y, z, c):
        x, y, z, c = lax.rem(x, 4), lax.rem(y, 4), lax.rem(z, 4), lax.rem(c, 2)
        return (x // 2) * 8 + z * 2 + c, y * 2 + lax.rem(x, 2)

    x_up, x_down, x_far = device(x + 1, y, z, c), device(x + 3, y, z, c), device(x + 2, y, z, c)
    y_up, y_down = device(x, y + 1, z, c), device(x, y + 3, z, c)
    z_up, z_down, z_far = device(x, y, z + 1, c), device(x, y, z + 3, c), device(x, y, z + 2, c)
    core = device(x, y, z, c + 1)
    x_pair = device(xh * 2 + 1 - xl, y, z, c)
    plane = [(step, side) for step in (2, 1, 3, 0) for side in (0, 1) if (step, side) != (0, 0)]

    locals_started = []

    def fetch(source, target):
        copy = pltpu.make_async_copy(source, target, local.at[len(locals_started)])
        copy.start()
        locals_started.append(copy)
        return copy

    def block_columns(ref, block):
        return ref.at[:, pl.ds(pl.multiple_of(block * rows, rows), rows)]

    def owner_columns(ref):
        return ref.at[:, pl.ds(pl.multiple_of(owner * width, width), width)]

    got_grad = fetch(kernel_grad, grad_tile)
    got_basis_out = fetch(basis_out, basis_out_tile)

    barrier = pltpu.get_barrier_semaphore()
    partners = [device(x + step, y, z, c + side) for step, side in plane]
    partners += [y_up, y_down, z_up, z_down, z_far]
    for partner in partners:
        pl.semaphore_signal(barrier, inc=1, device_id=partner, device_id_type=MESH)

    def strip_rows(x, y, c):
        block = (x // 2) * 2 + c
        start = pl.multiple_of((y * 2 + lax.rem(x, 2)) * strip, strip)
        return block, pl.ds(start, strip)

    my_block, my_rows = strip_rows(x, y, c)

    def basis_piece(t):
        return basis.at[my_block, my_rows, t * rows : (t + 1) * rows]

    own_basis = [
        fetch(block_columns(basis_in, xh * 8 + (2 * xl + t) * 2 + c), basis_piece(t)) for t in range(2)
    ]
    far, above, below = lax.rem(z + 2, 4), lax.rem(z + 1, 4), lax.rem(z + 3, 4)
    order = [far, above, below, z]
    got_tokens = {}
    got_columns = fetch(owner_columns(inputs), token_columns.at[0])
    got_grad_columns = fetch(owner_columns(grads), grad_columns.at[0])
    for step in range(4):
        for high in range(2):
            got_tokens[step, high] = fetch(
                block_columns(inputs, high * 8 + order[step] * 2 + c), tokens.at[0, step * 2 + high]
            )

    pl.semaphore_wait(barrier, len(partners))

    scatter_basis = []
    for step, side in plane:
        to_x = lax.rem(x + step, 4)
        to_c = lax.rem(c + side, 2)
        for t in range(2):
            block = (to_x // 2) * 8 + (2 * lax.rem(to_x, 2) + t) * 2 + to_c
            scatter_basis.append(
                Message(
                    pool,
                    block_columns(basis_in, block),
                    basis_piece(t),
                    device(x + step, y, z, c + side),
                ).start()
            )
    small = []
    for to in (z_up, z_down, z_far):
        small.append(Message(pool, eigen_in, eigen_rows.at[z], to).start())
    small.append(Message(pool, eigen_out, eigen_columns.at[xl], x_pair).start())

    token_messages = {}
    column_message = Message(pool, owner_columns(inputs), token_columns.at[1], core).start()
    for step in range(4):
        for high in range(2):
            token_messages[step, high] = Message(
                pool,
                block_columns(inputs, high * 8 + order[step] * 2 + 1 - c),
                tokens.at[1, step * 2 + high],
                core,
            ).start()
    grad_message = Message(pool, owner_columns(grads), grad_columns.at[1], core).start()

    got_grad.wait()
    got_basis_out.wait()

    def turned_tile(x, c):
        return turned.at[lax.rem(x, 2), (x // 2) * 2 + c]

    turned_tile(x, c)[...] = dot(grad_tile[...], basis_out_tile[...]).astype(BF16)
    half_rows = rows // 2

    def turned_region(place, half):
        return turned.at[lax.rem(place, 2), (place // 2) * 2 + c, half * half_rows : (half + 1) * half_rows]

    turned_gather = Gather(pool, turned_region, x, x_up, x_down)
    turned_gather.start(0)
    turned_gather.start(1)

    def to_core(step):
        tile = turned_tile(lax.rem(x + step, 4), c)
        return Message(pool, tile, tile, core).start()

    turned_core = [to_core(0)]

    for copy in own_basis:
        copy.wait()
    for message in scatter_basis:
        message.arrived()

    def basis_region(place, half):
        start = pl.multiple_of(place * 2 * strip, 2 * strip)
        return basis.at[half * 2 : half * 2 + 2, pl.ds(start, 2 * strip), :]

    basis_gather = Gather(pool, basis_region, y, y_up, y_down)
    basis_gather.start(0)
    basis_gather.start(1)

    def cov_mine(place, half):
        return cov.at[half, place]

    cov_scatter = Scatter(
        pool, cov_mine, lambda half: cov_transit.at[half], lambda slot: cov_slots.at[slot], z, z_up, z_down
    )
    got_columns.wait()
    got_grad_columns.wait()
    column_message.arrived()
    grad_message.arrived()
    grad_part[...] = (
        dot_rows(grad_columns[0], grad_columns[0]) + dot_rows(grad_columns[1], grad_columns[1])
    ).astype(BF16)

    def cov_product(step):
        for high in range(2):
            got_tokens[step, high].wait()
            token_messages[step, high].arrived()
        place = order[step]

        def product(high, unused):
            tile = dot_rows(tokens[0, step * 2 + high], token_columns[0])
            tile = tile + dot_rows(tokens[1, step * 2 + high], token_columns[1])
            cov[high, place, :rows] = tile.astype(BF16)
            start = pl.multiple_of((high * 8 + place * 2 + c) * out_rows, out_rows)
            cov[high, place, rows:] = grad_part[pl.ds(start, out_rows), :]
            return unused

        lax.fori_loop(0, 2, product, 0)

    cov_product(0)
    cov_scatter.start_far()
    turned_gather.forward()
    turned_gather.near()
    turned_core += [to_core(1), to_core(3)]
    basis_gather.forward()
    cov_product(1)
    cov_product(2)
    cov_scatter.start_near()
    cov_product(3)
    turned_gather.far()
    turned_core.append(to_core(2))
    basis_gather.near()
    basis_gather.far()
    for message in turned_core:
        message.arrived()

    def part_mine(place, half):
        return part.at[half, pl.ds(pl.multiple_of(place * narrow, narrow), narrow), :]

    part_scatter = Scatter(
        pool, part_mine, lambda half: part_transit.at[half], lambda slot: part_slots.at[slot], z, z_up, z_down
    )

    def rotate(t):
        start = pl.multiple_of(t * rows, rows)
        left = basis[:, :, pl.ds(start, rows)].reshape(4 * rows, rows)

        def one(side, unused):
            right = turned[side].reshape(4 * rows, width)
            part[side, pl.ds(start, rows), :] = dot_rows(left, right).astype(BF16)
            return unused

        lax.fori_loop(0, 2, one, 0)

    rotate(1 - z // 2)
    part_scatter.start_far()
    rotate(z // 2)
    part_scatter.start_near()

    for message in small:
        message.arrived()
    eigen_rows[z] = eigen_in[...]
    eigen_columns[xl] = eigen_out[...]
    line = eigen_rows[2 * xl + z // 2]
    line = jnp.where(lax.rem(z, 2) == 0, line[:, :narrow], line[:, narrow:])
    column = jnp.transpose(jnp.broadcast_to(line[:1], (128, narrow)))[:, :1]

    part_scatter.forward()

    def scaled_region(place, half):
        return scaled.at[half, pl.ds(pl.multiple_of(place * narrow, narrow), narrow), :]

    scaled_gather = Gather(pool, scaled_region, z, z_up, z_down)
    for half in range(2):
        part_scatter.arrived(half)
        divisor = column * eigen_columns[half][:1] + damping
        scaled_region(z, half)[...] = (part_scatter.total(half) / divisor).astype(BF16)
        scaled_gather.start(half)
    scaled_gather.forward()
    cov_scatter.forward()
    scaled_gather.near()
    scaled_gather.far()

    lines = rows // CHUNKS
    half_width = width // 2
    half_lines = lines // 2
    finishing = []
    scatters = []
    for chunk in range(CHUNKS):
        chunk_rows = slice(chunk * lines, (chunk + 1) * lines)

        def partial(side, target):
            def one(place, unused):
                left = basis[(place // 2) * 2 + side, chunk_rows, :]
                target[place] = dot(left, scaled[lax.rem(place, 2)]).astype(target.dtype)
                return unused

            lax.fori_loop(0, 4, one, 0)

        partial(1 - c, away.at[chunk])
        crossing = Message(pool, away.at[chunk], away_in.at[chunk], core).start()
        finishing.append(crossing)
        partial(c, home)
        crossing.arrived()
        home_sum[chunk] = (home[...] + away_in[chunk].astype(F32)).astype(BF16)

        def home_mine(place, half, chunk=chunk):
            return home_sum.at[chunk, place, :, half * half_width : (half + 1) * half_width]

        scatter = Scatter(
            pool,
            home_mine,
            lambda half, chunk=chunk: home_transit.at[chunk, half],
            lambda slot, chunk=chunk: home_slots.at[chunk, slot],
            x,
            x_up,
            x_down,
        )
        scatter.start_far()
        scatter.start_near()
        scatters.append(scatter)

    ends = []
    for chunk in range(CHUNKS):
        scatter = scatters[chunk]
        scatter.forward()
        scatter.arrived(0)
        scatter.arrived(1)
        restored = jnp.concatenate([scatter.total(0), scatter.total(1)], axis=1).astype(BF16)
        new = lax.dot_general(restored, basis_out_tile[...], (((1,), (1,)), ((), ())), preferred_element_type=F32)

        def region(place, half, high, chunk=chunk):
            start = (high * 8 + place * 2 + c) * rows + chunk * lines
            if half is None:
                return gathered.at[pl.ds(pl.multiple_of(start, 16), lines), :]
            return gathered.at[pl.ds(pl.multiple_of(start + half * half_lines, 16), half_lines), :]

        own_gather = Gather(pool, functools.partial(region, high=xh), z, z_up, z_down)
        other_gather = Gather(pool, functools.partial(region, high=1 - xh), z, z_up, z_down)
        mine = region(z, None, xh)
        mine[...] = new.astype(BF16)
        own_gather.start(0)
        own_gather.start(1)
        across = Message(pool, mine, mine, x_far).start()
        finishing += [across, Message(pool, mine, mine, core).start()]
        ends.append((own_gather, other_gather, across, region))

    cov_scatter.arrived(0)
    cov_scatter.arrived(1)
    totals = [cov_scatter.total(0), cov_scatter.total(1)]
    cov[1 - xh, z] = jnp.where(xh == 0, totals[1], totals[0]).astype(BF16)
    cov_message = Message(pool, cov.at[1 - xh, z], cov_across, x_far).start()

    to_core_last = []
    for own_gather, other_gather, across, region in ends:
        across.arrived()
        other_gather.start(0)
        other_gather.start(1)
        received = region(z, None, 1 - xh)
        to_core_last.append(Message(pool, received, received, core).start())
    for own_gather, other_gather, across, region in ends:
        for gather, high in ((own_gather, xh), (other_gather, 1 - xh)):
            gather.forward()
            gather.near()
            for place in (above, below):
                received = region(place, None, high)
                to_core_last.append(Message(pool, received, received, core).start())

    cov_message.arrived()
    total = jnp.where(xh == 0, totals[0], totals[1]) + cov_across[...].astype(F32)
    in_cov[...] = total[:rows]
    out_cov[...] = total[rows:]

    for own_gather, other_gather, across, region in ends:
        for gather, high in ((own_gather, xh), (other_gather, 1 - xh)):
            gather.far()
            received = region(far, None, high)
            to_core_last.append(Message(pool, received, received, core).start())

    for message in to_core_last:
        message.arrived()
    for own_gather, other_gather, across, region in ends:
        own_gather.sent()
        other_gather.sent()
    for chunk, message in enumerate(finishing[CHUNKS:]):
        if chunk % 2 == 1:
            message.arrived()
    for message in finishing + to_core_last + scatter_basis + small + turned_core:
        message.sent()
    for message in list(token_messages.values()) + [column_message, grad_message, cov_message]:
        message.sent()
    for group in [turned_gather, basis_gather, scaled_gather, cov_scatter, part_scatter] + scatters:
        group.sent()


def finish(gathered, in_cov, out_cov, old_in, old_out, precond, in_factor, out_factor, sem, tokens):
    copy = pltpu.make_async_copy(gathered, precond, sem)
    copy.start()
    in_factor[...] = factor_decay * old_in[...] + (1.0 - factor_decay) * in_cov[...] / tokens
    out_factor[...] = factor_decay * old_out[...] + (1.0 - factor_decay) * out_cov[...] / tokens
    copy.wait()


def shards(
    inputs, out_grads, kernel_grad, basis_in, basis_out, eigen_in, eigen_out, old_in_factor, old_out_factor
):
    rows, width = kernel_grad.shape
    strip = basis_in.shape[0]
    tokens = inputs.shape[0]
    out_rows = old_out_factor.shape[0]
    deep = rows + out_rows
    total = 16 * rows
    lines = rows // CHUNKS
    narrow = width // 4
    anywhere = pl.BlockSpec(memory_space=pl.ANY)
    vmem = pl.BlockSpec(memory_space=pltpu.VMEM)
    scratch = [
        pltpu.VMEM((4, rows, 2 * rows), BF16),
        pltpu.VMEM((2, 4, rows, width), BF16),
        pltpu.VMEM((2, 4 * narrow, width), BF16),
        pltpu.VMEM((2, narrow, width), BF16),
        pltpu.VMEM((4, narrow, width), BF16),
        pltpu.VMEM((2, 4 * narrow, width), BF16),
        pltpu.VMEM((4, 8, rows), F32),
        pltpu.VMEM((2, 8, width), F32),
        pltpu.VMEM((CHUNKS, 4, lines, width), BF16),
        pltpu.VMEM((CHUNKS, 4, lines, width), BF16),
        pltpu.VMEM((4, lines, width), F32),
        pltpu.VMEM((CHUNKS, 4, lines, width), BF16),
        pltpu.VMEM((CHUNKS, 2, lines, width // 2), BF16),
        pltpu.VMEM((CHUNKS, 4, lines, width // 2), BF16),
        pltpu.VMEM((2, 8, tokens, rows), BF16),
        pltpu.VMEM((2, tokens, width), BF16),
        pltpu.VMEM((2, tokens, width), BF16),
        pltpu.VMEM((width, width), BF16),
        pltpu.VMEM((2, 4, deep, width), BF16),
        pltpu.VMEM((2, deep, width), BF16),
        pltpu.VMEM((4, deep, width), BF16),
        pltpu.VMEM((deep, width), BF16),
        pltpu.VMEM((rows, width), BF16),
        pltpu.VMEM((width, width), BF16),
        pltpu.SemaphoreType.DMA((16,)),
        pltpu.SemaphoreType.DMA((MESSAGES,)),
        pltpu.SemaphoreType.DMA((MESSAGES,)),
    ]
    gathered, in_cov, out_cov = pl.pallas_call(
        kernel,
        out_shape=(
            pltpu.VMEM((total, width), BF16),
            jax.ShapeDtypeStruct((rows, width), F32),
            jax.ShapeDtypeStruct((out_rows, width), F32),
        ),
        in_specs=[anywhere] * 5 + [vmem] * 2,
        out_specs=(vmem, vmem, vmem),
        scratch_shapes=scratch,
        compiler_params=pltpu.CompilerParams(
            collective_id=0, has_side_effects=True, vmem_limit_bytes=52 * 2**20
        ),
        cost_estimate=pl.CostEstimate(flops=2 * 10**10, bytes_accessed=4 * 10**7, transcendentals=0),
        name="precondition",
    )(
        inputs,
        out_grads,
        kernel_grad,
        basis_in,
        basis_out,
        jnp.broadcast_to(eigen_in[None, :], (8, rows)),
        jnp.broadcast_to(eigen_out[None, :], (8, width)),
    )
    return pl.pallas_call(
        functools.partial(finish, tokens=16 * tokens),
        out_shape=(
            jax.ShapeDtypeStruct((total, width), BF16),
            jax.ShapeDtypeStruct((rows, width), F32),
            jax.ShapeDtypeStruct((out_rows, width), F32),
        ),
        in_specs=[vmem] * 5,
        out_specs=(anywhere, vmem, vmem),
        scratch_shapes=[pltpu.SemaphoreType.DMA],
        compiler_params=pltpu.CompilerParams(vmem_limit_bytes=40 * 2**20),
        name="finish",
    )(gathered, in_cov, out_cov, old_in_factor, old_out_factor)


def solution(mesh):
    in_specs = (
        P("dp", None),
        P("dp", None),
        P("dp", "owner"),
        P(("dp", "owner"), None),
        P("owner", None),
        P("dp"),
        P("owner"),
        P("dp", "owner"),
        P(("owner", "dp"), None),
    )
    out_specs = (P(None, "owner"), P("dp", "owner"), P(("owner", "dp"), None))
    return jax.shard_map(shards, mesh=mesh, in_specs=in_specs, out_specs=out_specs, check_vma=False)
```

```python
import functools

import jax
import jax.numpy as jnp
from jax import lax
from jax.experimental import pallas as pl
from jax.experimental.pallas import tpu as pltpu
from jax.sharding import PartitionSpec as P

damping = 0.3
factor_decay = 0.9
MESH = pl.DeviceIdType.MESH
CHUNKS = 3
WAVES = 2
MESSAGES = 256
F32 = jnp.float32
BF16 = jnp.bfloat16


def dot_rows(left, right):
    return lax.dot_general(left, right, (((0,), (0,)), ((), ())), preferred_element_type=F32)


def dot(left, right):
    return jnp.dot(left, right, preferred_element_type=F32)


class Message:
    def __init__(self, pool, source, target, to):
        number = pool[2]
        pool[2] += 1
        self.copy = pltpu.make_async_remote_copy(
            src_ref=source,
            dst_ref=target,
            send_sem=pool[0].at[number],
            recv_sem=pool[1].at[number],
            device_id=to,
            device_id_type=MESH,
        )

    def start(self):
        self.copy.start()
        return self

    def arrived(self):
        self.copy.wait_recv()

    def sent(self):
        self.copy.wait_send()


class Gather:
    def __init__(self, pool, region, place, plus, minus):
        self.region, self.place, self.plus, self.minus, self.pool = region, place, plus, minus, pool
        self.own = {}
        self.passed = []

    def message(self, shard, half, to):
        piece = self.region(shard, half)
        return Message(self.pool, piece, piece, to).start()

    def start(self, half):
        order = (("plus", self.plus), ("minus", self.minus))
        for name, to in order if half == 0 else order[::-1]:
            self.own[name, half] = self.message(self.place, half, to)

    def forward(self):
        below, above = lax.rem(self.place + 3, 4), lax.rem(self.place + 1, 4)
        self.own["plus", 0].arrived()
        self.passed.append(self.message(below, 0, self.plus))
        self.own["minus", 1].arrived()
        self.passed.append(self.message(above, 1, self.minus))

    def near(self):
        self.own["minus", 0].arrived()
        self.own["plus", 1].arrived()

    def far(self):
        for message in self.passed:
            message.arrived()

    def sent(self):
        for message in list(self.own.values()) + self.passed:
            message.sent()


class Scatter:
    def __init__(self, pool, mine, transit, slots, place, plus, minus):
        self.pool, self.mine, self.transit, self.slots = pool, mine, transit, slots
        self.plus, self.minus = plus, minus
        self.here = place
        self.above, self.below, self.far = (lax.rem(place + step, 4) for step in (1, 3, 2))
        self.messages = []

    def send(self, source, target, to):
        message = Message(self.pool, source, target, to).start()
        self.messages.append(message)
        return message

    def start_far(self):
        self.up = self.send(self.mine(self.far, 0), self.transit(0), self.plus)
        self.down = self.send(self.mine(self.far, 1), self.transit(1), self.minus)

    def start_near(self):
        self.direct_up = self.send(self.mine(self.above, 1), self.slots(0), self.plus)
        self.direct_down = self.send(self.mine(self.below, 0), self.slots(1), self.minus)

    def add(self):
        for message, half, place in ((self.up, 0, self.above), (self.down, 1, self.below)):
            message.arrived()
            piece = self.mine(place, half)
            piece[...] = (piece[...].astype(F32) + self.transit(half)[...].astype(F32)).astype(BF16)
            if half == 0:
                self.pass_up()
        self.pass_down()

    def pass_up(self):
        self.sum_up = self.send(self.mine(self.above, 0), self.slots(2), self.plus)

    def pass_down(self):
        self.sum_down = self.send(self.mine(self.below, 1), self.slots(3), self.minus)

    def arrived(self, half):
        if half == 0:
            self.direct_down.arrived()
            self.sum_up.arrived()
        else:
            self.direct_up.arrived()
            self.sum_down.arrived()

    def total(self, half):
        return (
            self.mine(self.here, half)[...].astype(F32)
            + self.slots(1 - half)[...].astype(F32)
            + self.slots(2 + half)[...].astype(F32)
        )

    def sent(self):
        for message in self.messages:
            message.sent()


def kernel(
    inputs,
    grads,
    kernel_grad,
    basis_in,
    basis_out,
    eigen_in,
    eigen_out,
    gathered,
    in_cov,
    out_cov,
    basis,
    turned,
    part,
    part_transit,
    part_slots,
    scaled,
    eigen_rows,
    eigen_columns,
    away,
    away_in,
    home,
    home_sum,
    restored_part,
    home_transit,
    home_slots,
    tokens,
    token_columns,
    grad_columns,
    grad_part,
    cov,
    cov_transit,
    cov_slots,
    cov_across,
    grad_tile,
    basis_out_tile,
    local,
    send,
    receive,
):
    pool = [send, receive, 0]
    rows = kernel_grad.shape[0]
    width = kernel_grad.shape[1]
    strip = basis_in.shape[0]
    out_rows = out_cov.shape[0]
    narrow = width // 4
    dp, owner = lax.axis_index("dp"), lax.axis_index("owner")
    xh, z, c = dp // 8, lax.rem(dp // 2, 4), lax.rem(dp, 2)
    y, xl = owner // 2, lax.rem(owner, 2)
    x = xh * 2 + xl

    def device(x, y, z, c):
        x, y, z, c = lax.rem(x, 4), lax.rem(y, 4), lax.rem(z, 4), lax.rem(c, 2)
        return (x // 2) * 8 + z * 2 + c, y * 2 + lax.rem(x, 2)

    x_up, x_down, x_far = device(x + 1, y, z, c), device(x + 3, y, z, c), device(x + 2, y, z, c)
    y_up, y_down = device(x, y + 1, z, c), device(x, y + 3, z, c)
    z_up, z_down, z_far = device(x, y, z + 1, c), device(x, y, z + 3, c), device(x, y, z + 2, c)
    core = device(x, y, z, c + 1)
    pair = xh * 2 + 1 - xl
    cross = lax.rem(x + 2 * xl + 3, 4)
    plane = [(step, side) for step in (-1, 0, -2, 2) for side in (0, 1) if (step, side) != (0, 0)]
    x_pair = device(pair, y, z, c)

    locals_started = []

    def fetch(source, target):
        copy = pltpu.make_async_copy(source, target, local.at[len(locals_started)])
        copy.start()
        locals_started.append(copy)
        return copy

    def block_columns(ref, block):
        return ref.at[:, pl.ds(pl.multiple_of(block * rows, rows), rows)]

    def owner_columns(ref):
        return ref.at[:, pl.ds(pl.multiple_of(owner * width, width), width)]

    got_grad = fetch(kernel_grad, grad_tile)
    got_basis_out = fetch(basis_out, basis_out_tile)

    barrier = pltpu.get_barrier_semaphore()
    partners = [device(x + step, y, z, c + side) for step in range(4) for side in range(2) if step + side > 0]
    partners += [y_up, y_down, z_up, z_down, z_far]
    for partner in partners:
        pl.semaphore_signal(barrier, inc=1, device_id=partner, device_id_type=MESH)

    def strip_rows(x, y, c):
        block = (x // 2) * 2 + c
        start = pl.multiple_of((y * 2 + lax.rem(x, 2)) * strip, strip)
        return block, pl.ds(start, strip)

    my_block, my_rows = strip_rows(x, y, c)

    def basis_piece(t):
        return basis.at[my_block, my_rows, t * rows : (t + 1) * rows]

    own_basis = [
        fetch(block_columns(basis_in, xh * 8 + (2 * xl + t) * 2 + c), basis_piece(t)) for t in range(2)
    ]
    far, above, below = lax.rem(z + 2, 4), lax.rem(z + 1, 4), lax.rem(z + 3, 4)
    order = [far, above, below, z]
    got_tokens = {}
    got_columns = fetch(owner_columns(inputs), token_columns.at[0])
    got_grad_columns = fetch(owner_columns(grads), grad_columns.at[0])
    for step in range(4):
        for high in range(2):
            got_tokens[step, high] = fetch(
                block_columns(inputs, high * 8 + order[step] * 2 + c), tokens.at[0, step * 2 + high]
            )

    pl.semaphore_wait(barrier, len(partners))

    scatter_basis = {}
    for step, side in plane:
        to = {-1: pair, -2: cross, 0: x, 2: lax.rem(x + 2, 4)}[step]
        to_c = lax.rem(c + side, 2)
        for t in range(2):
            block = (to // 2) * 8 + (2 * lax.rem(to, 2) + t) * 2 + to_c
            scatter_basis[step, side, t] = Message(
                pool, block_columns(basis_in, block), basis_piece(t), device(to, y, z, to_c)
            ).start()
    small = []
    eigen_rows[z] = jnp.broadcast_to(eigen_in[...].reshape(1, rows), (8, rows))
    eigen_columns[xl] = jnp.broadcast_to(eigen_out[...].reshape(1, width), (8, width))
    for to in (z_up, z_down, z_far):
        small.append(Message(pool, eigen_rows.at[z], eigen_rows.at[z], to).start())
    small.append(Message(pool, eigen_columns.at[xl], eigen_columns.at[xl], x_pair).start())

    token_messages = {}
    column_message = Message(pool, owner_columns(inputs), token_columns.at[1], core).start()
    for step in range(4):
        for high in range(2):
            token_messages[step, high] = Message(
                pool,
                block_columns(inputs, high * 8 + order[step] * 2 + 1 - c),
                tokens.at[1, step * 2 + high],
                core,
            ).start()
    grad_message = Message(pool, owner_columns(grads), grad_columns.at[1], core).start()

    got_grad.wait()
    got_basis_out.wait()

    def turned_tile(x, c):
        return turned.at[lax.rem(x, 2), (x // 2) * 2 + c]

    turned_tile(x, c)[...] = dot(grad_tile[...], basis_out_tile[...]).astype(BF16)
    half_rows = rows // 2

    def turned_region(place, half):
        return turned.at[lax.rem(place, 2), (place // 2) * 2 + c, half * half_rows : (half + 1) * half_rows]

    def to_core(step):
        tile = turned_tile(lax.rem(x + step, 4), c)
        return Message(pool, tile, tile, core).start()

    turned_gather = Gather(pool, turned_region, x, x_up, x_down)

    def basis_region(place, half):
        start = pl.multiple_of(place * 2 * strip, 2 * strip)
        high = 2 * lax.rem(xh + half, 2)
        return basis.at[pl.ds(high, 2), pl.ds(start, 2 * strip), :]

    basis_gather = Gather(pool, basis_region, y, y_up, y_down)
    for copy in own_basis:
        copy.wait()
    for (step, side, t), message in scatter_basis.items():
        if step in (-1, 0):
            message.arrived()
    basis_gather.start(0)
    turned_gather.start(0)
    for (step, side, t), message in scatter_basis.items():
        if step not in (-1, 0):
            message.arrived()
    basis_gather.start(1)
    turned_gather.start(1)
    turned_core = [to_core(0)]

    def cov_mine(place, half):
        return cov.at[half, place]

    cov_scatter = Scatter(
        pool, cov_mine, lambda half: cov_transit.at[half], lambda slot: cov_slots.at[slot], z, z_up, z_down
    )
    got_columns.wait()
    got_grad_columns.wait()
    column_message.arrived()
    grad_message.arrived()
    grad_part[...] = (
        dot_rows(grad_columns[0], grad_columns[0]) + dot_rows(grad_columns[1], grad_columns[1])
    ).astype(BF16)

    def cov_product(step):
        for high in range(2):
            got_tokens[step, high].wait()
            token_messages[step, high].arrived()
        place = order[step]

        def product(high, unused):
            tile = dot_rows(tokens[0, step * 2 + high], token_columns[0])
            tile = tile + dot_rows(tokens[1, step * 2 + high], token_columns[1])
            cov[high, place, :rows] = tile.astype(BF16)
            start = pl.multiple_of((high * 8 + place * 2 + c) * out_rows, out_rows)
            cov[high, place, rows:] = grad_part[pl.ds(start, out_rows), :]
            return unused

        lax.fori_loop(0, 2, product, 0)

    cov_product(0)
    cov_scatter.start_far()
    turned_gather.forward()
    turned_gather.near()
    turned_core += [to_core(1), to_core(3)]
    basis_gather.forward()
    cov_product(1)
    cov_product(2)
    cov_scatter.start_near()
    cov_product(3)
    turned_gather.far()
    turned_core.append(to_core(2))
    basis_gather.near()
    basis_gather.far()
    for message in turned_core:
        message.arrived()

    wave = width // WAVES

    def rows_of(ref, place, half, number):
        start = pl.multiple_of(place * narrow, narrow)
        return ref.at[half, pl.ds(start, narrow), number * wave : (number + 1) * wave]

    part_scatters = [
        Scatter(
            pool,
            lambda place, half, number=number: rows_of(part, place, half, number),
            lambda half, number=number: part_transit.at[number, half],
            lambda slot, number=number: part_slots.at[number, slot],
            z,
            z_up,
            z_down,
        )
        for number in range(WAVES)
    ]

    def rotate(t, number):
        start = pl.multiple_of(t * rows, rows)
        left = basis[:, :, pl.ds(start, rows)].reshape(4 * rows, rows)

        def one(side, unused):
            right = turned[side, :, :, number * wave : (number + 1) * wave].reshape(4 * rows, wave)
            part[side, pl.ds(start, rows), number * wave : (number + 1) * wave] = dot_rows(left, right).astype(BF16)
            return unused

        lax.fori_loop(0, 2, one, 0)

    for number, scatter in enumerate(part_scatters):
        rotate(1 - z // 2, number)
        scatter.start_far()
        if number > 0:
            part_scatters[number - 1].add()
        rotate(z // 2, number)
        scatter.start_near()

    for message in small:
        message.arrived()
    line = eigen_rows[2 * xl + z // 2]
    line = jnp.where(lax.rem(z, 2) == 0, line[:, :narrow], line[:, narrow:])
    column = jnp.transpose(jnp.broadcast_to(line[:1], (128, narrow)))[:, :1]

    scaled_gathers = []
    for number, scatter in enumerate(part_scatters):
        gather = Gather(
            pool, lambda place, half, number=number: rows_of(scaled, place, half, number), z, z_up, z_down
        )
        for half in range(2):
            scatter.arrived(half)
            divisor = column * eigen_columns[half, :1, number * wave : (number + 1) * wave] + damping
            rows_of(scaled, z, half, number)[...] = (scatter.total(half) / divisor).astype(BF16)
            gather.start(half)
        scaled_gathers.append(gather)
        if number + 1 < WAVES:
            if number + 2 == WAVES:
                part_scatters[number + 1].add()
            gather.forward()

    lines = rows // CHUNKS
    half_lines = lines // 2
    crossings, sums, ends, to_core_last = [], [], [], []

    def pass_to_core(ref):
        to_core_last.append(Message(pool, ref, ref, core).start())

    def start_sum(number):
        def partial(side, target):
            def one(place, unused):
                left = basis[(place // 2) * 2 + side]
                right = scaled[lax.rem(place, 2), :, number * wave : (number + 1) * wave]
                target[place] = dot(left, right).astype(target.dtype)
                return unused

            lax.fori_loop(0, 4, one, 0)

        partial(1 - c, away.at[number])
        crossings.append(Message(pool, away.at[number], away_in.at[number], core).start())
        partial(c, home)

    def cross_sum(number, count):
        crossings[number].arrived()
        home_sum[number] = (home[...] + away_in[number].astype(F32)).astype(BF16)
        size = rows // count // 2
        for chunk in range(count):
            sums.append(
                Scatter(
                    pool,
                    lambda place, half, start=chunk * 2 * size: home_sum.at[
                        number, place, start + half * size : start + (half + 1) * size, :
                    ],
                    lambda half, start=chunk * size: home_transit.at[number, half, start : start + size, :],
                    lambda slot, start=chunk * size: home_slots.at[number, slot, start : start + size, :],
                    x,
                    x_up,
                    x_down,
                )
            )

    def finish_sum(scatter):
        scatter.arrived(0)
        scatter.arrived(1)
        return jnp.concatenate([scatter.total(0), scatter.total(1)], axis=0).astype(BF16)

    for number, gather in enumerate(scaled_gathers):
        gather.near()
        gather.far()
        start_sum(number)
        if number + 1 < WAVES:
            scaled_gathers[number + 1].forward()
            cross_sum(number, 1)
            sums[number].start_far()
            sums[number].start_near()
            if number + 2 == WAVES:
                cov_scatter.add()
        else:
            for before in sums:
                before.add()
            cross_sum(number, CHUNKS)
    last_sums = sums[WAVES - 1 :]
    last_sums[0].start_far()
    last_sums[0].start_near()
    if CHUNKS > 1:
        last_sums[1].start_far()
    for number in range(WAVES - 1):
        restored_part[:, number * wave : (number + 1) * wave] = finish_sum(sums[number])

    def finish_chunk(chunk):
        chunk_rows = slice(chunk * lines, (chunk + 1) * lines)
        restored_part[chunk_rows, (WAVES - 1) * wave :] = finish_sum(last_sums[chunk])
        new = lax.dot_general(
            restored_part[chunk_rows, :],
            basis_out_tile[...],
            (((1,), (1,)), ((), ())),
            preferred_element_type=F32,
        )

        def region(place, half, high):
            start = (high * 8 + place * 2 + c) * rows + chunk * lines
            if half is None:
                return gathered.at[pl.ds(pl.multiple_of(start, 16), lines), :]
            return gathered.at[pl.ds(pl.multiple_of(start + half * half_lines, 16), half_lines), :]

        own = Gather(pool, functools.partial(region, high=xh), z, z_up, z_down)
        other = Gather(pool, functools.partial(region, high=1 - xh), z, z_up, z_down)
        mine = region(z, None, xh)
        mine[...] = new.astype(BF16)
        across = Message(pool, mine, mine, x_far).start()
        own.start(0)
        own.start(1)
        pass_to_core(mine)
        ends.append((own, other, across, region))

    def start_other(chunk):
        own, other, across, region = ends[chunk]
        across.arrived()
        other.start(0)
        other.start(1)
        pass_to_core(region(z, None, 1 - xh))

    def forward(chunk, high):
        gather = ends[chunk][high]
        region = ends[chunk][3]
        gather.forward()
        gather.near()
        for place in (above, below):
            pass_to_core(region(place, None, xh if high == 0 else 1 - xh))

    def last(chunk, high):
        ends[chunk][high].far()
        pass_to_core(ends[chunk][3](far, None, xh if high == 0 else 1 - xh))

    last_sums[0].add()
    for chunk in range(CHUNKS):
        if chunk + 1 < CHUNKS:
            last_sums[chunk + 1].start_near()
        if chunk + 2 < CHUNKS:
            last_sums[chunk + 2].start_far()
        finish_chunk(chunk)
        if chunk + 1 < CHUNKS:
            last_sums[chunk + 1].add()
        if chunk >= 1:
            forward(chunk - 1, 0)
            start_other(chunk - 1)
        if chunk >= 2:
            forward(chunk - 2, 1)
    forward(CHUNKS - 1, 0)
    start_other(CHUNKS - 1)
    if CHUNKS > 1:
        forward(CHUNKS - 2, 1)

    cov_scatter.arrived(0)
    cov_scatter.arrived(1)
    cov[1 - xh, z] = cov_scatter.total(1 - xh).astype(BF16)
    cov_message = Message(pool, cov.at[1 - xh, z], cov_across, x_far).start()

    forward(CHUNKS - 1, 1)
    for chunk in range(CHUNKS):
        last(chunk, 0)
    total = cov_scatter.total(xh)
    for chunk in range(CHUNKS):
        last(chunk, 1)
    cov_message.arrived()
    total = total + cov_across[...].astype(F32)
    in_cov[...] = total[:rows]
    out_cov[...] = total[rows:]

    for message in to_core_last:
        message.arrived()
    for own, other, across, region in ends:
        own.sent()
        other.sent()
        across.sent()
    for message in crossings + to_core_last + list(scatter_basis.values()) + small + turned_core:
        message.sent()
    for message in list(token_messages.values()) + [column_message, grad_message, cov_message]:
        message.sent()
    for group in [turned_gather, basis_gather, cov_scatter] + part_scatters + scaled_gathers + sums:
        group.sent()


def finish(gathered, in_cov, out_cov, old_in, old_out, precond, in_factor, out_factor, new_in, new_out, sem, tokens):
    copies = [pltpu.make_async_copy(gathered, precond, sem.at[0])]
    copies[0].start()
    new_in[...] = factor_decay * old_in[...] + (1.0 - factor_decay) * in_cov[...] / tokens
    new_out[...] = factor_decay * old_out[...] + (1.0 - factor_decay) * out_cov[...] / tokens
    copies += [pltpu.make_async_copy(new_in, in_factor, sem.at[1])]
    copies += [pltpu.make_async_copy(new_out, out_factor, sem.at[2])]
    for copy in copies[1:]:
        copy.start()
    for copy in copies:
        copy.wait()


def shards(
    inputs, out_grads, kernel_grad, basis_in, basis_out, eigen_in, eigen_out, old_in_factor, old_out_factor
):
    rows, width = kernel_grad.shape
    strip = basis_in.shape[0]
    tokens = inputs.shape[0]
    out_rows = old_out_factor.shape[0]
    deep = rows + out_rows
    total = 16 * rows
    narrow = width // 4
    anywhere = pl.BlockSpec(memory_space=pl.ANY)
    vmem = pl.BlockSpec(memory_space=pltpu.VMEM)
    scratch = [
        pltpu.VMEM((4, rows, 2 * rows), BF16),
        pltpu.VMEM((2, 4, rows, width), BF16),
        pltpu.VMEM((2, 4 * narrow, width), BF16),
        pltpu.VMEM((WAVES, 2, narrow, width // WAVES), BF16),
        pltpu.VMEM((WAVES, 4, narrow, width // WAVES), BF16),
        pltpu.VMEM((2, 4 * narrow, width), BF16),
        pltpu.VMEM((4, 8, rows), F32),
        pltpu.VMEM((2, 8, width), F32),
        pltpu.VMEM((WAVES, 4, rows, width // WAVES), BF16),
        pltpu.VMEM((WAVES, 4, rows, width // WAVES), BF16),
        pltpu.VMEM((4, rows, width // WAVES), F32),
        pltpu.VMEM((WAVES, 4, rows, width // WAVES), BF16),
        pltpu.VMEM((rows, width), BF16),
        pltpu.VMEM((WAVES, 2, rows // 2, width // WAVES), BF16),
        pltpu.VMEM((WAVES, 4, rows // 2, width // WAVES), BF16),
        pltpu.VMEM((2, 8, tokens, rows), BF16),
        pltpu.VMEM((2, tokens, width), BF16),
        pltpu.VMEM((2, tokens, width), BF16),
        pltpu.VMEM((width, width), BF16),
        pltpu.VMEM((2, 4, deep, width), BF16),
        pltpu.VMEM((2, deep, width), BF16),
        pltpu.VMEM((4, deep, width), BF16),
        pltpu.VMEM((deep, width), BF16),
        pltpu.VMEM((rows, width), BF16),
        pltpu.VMEM((width, width), BF16),
        pltpu.SemaphoreType.DMA((16,)),
        pltpu.SemaphoreType.DMA((MESSAGES,)),
        pltpu.SemaphoreType.DMA((MESSAGES,)),
    ]
    gathered, in_cov, out_cov = pl.pallas_call(
        kernel,
        out_shape=(
            pltpu.VMEM((total, width), BF16),
            pltpu.VMEM((rows, width), F32),
            pltpu.VMEM((out_rows, width), F32),
        ),
        in_specs=[anywhere] * 5 + [vmem] * 2,
        out_specs=(vmem, vmem, vmem),
        scratch_shapes=scratch,
        compiler_params=pltpu.CompilerParams(
            collective_id=0, has_side_effects=True, vmem_limit_bytes=52 * 2**20
        ),
        cost_estimate=pl.CostEstimate(flops=2 * 10**10, bytes_accessed=4 * 10**7, transcendentals=0),
        name="precondition",
    )(
        inputs,
        out_grads,
        kernel_grad,
        basis_in,
        basis_out,
        eigen_in,
        eigen_out,
    )
    return pl.pallas_call(
        functools.partial(finish, tokens=16 * tokens),
        out_shape=(
            jax.ShapeDtypeStruct((total, width), BF16),
            jax.ShapeDtypeStruct((rows, width), F32),
            jax.ShapeDtypeStruct((out_rows, width), F32),
        ),
        in_specs=[vmem] * 5,
        out_specs=(anywhere, anywhere, anywhere),
        scratch_shapes=[pltpu.VMEM((rows, width), F32), pltpu.VMEM((out_rows, width), F32), pltpu.SemaphoreType.DMA((3,))],
        compiler_params=pltpu.CompilerParams(vmem_limit_bytes=40 * 2**20),
        name="finish",
    )(gathered, in_cov, out_cov, old_in_factor, old_out_factor)


def solution(mesh):
    in_specs = (
        P("dp", None),
        P("dp", None),
        P("dp", "owner"),
        P(("dp", "owner"), None),
        P("owner", None),
        P("dp"),
        P("owner"),
        P("dp", "owner"),
        P(("owner", "dp"), None),
    )
    out_specs = (P(None, "owner"), P("dp", "owner"), P(("owner", "dp"), None))
    return jax.shard_map(shards, mesh=mesh, in_specs=in_specs, out_specs=out_specs, check_vma=False)
```

```python
import functools

import jax
import jax.numpy as jnp
from jax import lax
from jax.experimental import pallas as pl
from jax.experimental.pallas import tpu as pltpu
from jax.sharding import PartitionSpec as P

damping = 0.3
factor_decay = 0.9
MESH = pl.DeviceIdType.MESH
CHUNKS = 3
WAVES = 2
MESSAGES = 256
F32 = jnp.float32
BF16 = jnp.bfloat16


def dot_rows(left, right):
    return lax.dot_general(left, right, (((0,), (0,)), ((), ())), preferred_element_type=F32)


def dot(left, right):
    return jnp.dot(left, right, preferred_element_type=F32)


class Message:
    def __init__(self, pool, source, target, to):
        number = pool[2]
        pool[2] += 1
        self.sems = (pool[0].at[number], pool[1].at[number])
        self.copy = pltpu.make_async_remote_copy(
            src_ref=source,
            dst_ref=target,
            send_sem=pool[0].at[number],
            recv_sem=pool[1].at[number],
            device_id=to,
            device_id_type=MESH,
        )

    def start(self):
        self.copy.start()
        return self

    def arrived(self):
        self.copy.wait_recv()

    def sent(self):
        self.copy.wait_send()


class Gather:
    def __init__(self, pool, region, place, plus, minus):
        self.region, self.place, self.plus, self.minus, self.pool = region, place, plus, minus, pool
        self.own = {}
        self.passed = []

    def message(self, shard, half, to):
        piece = self.region(shard, half)
        return Message(self.pool, piece, piece, to).start()

    def start(self, half):
        order = (("plus", self.plus), ("minus", self.minus))
        for name, to in order if half == 0 else order[::-1]:
            self.own[name, half] = self.message(self.place, half, to)

    def forward(self):
        below, above = lax.rem(self.place + 3, 4), lax.rem(self.place + 1, 4)
        self.own["plus", 0].arrived()
        self.passed.append(self.message(below, 0, self.plus))
        self.own["minus", 1].arrived()
        self.passed.append(self.message(above, 1, self.minus))

    def near(self):
        self.own["minus", 0].arrived()
        self.own["plus", 1].arrived()

    def far(self):
        for message in self.passed:
            message.arrived()

    def sent(self):
        for message in list(self.own.values()) + self.passed:
            message.sent()


class Scatter:
    def __init__(self, pool, mine, transit, slots, place, plus, minus):
        self.pool, self.mine, self.transit, self.slots = pool, mine, transit, slots
        self.plus, self.minus = plus, minus
        self.here = place
        self.above, self.below, self.far = (lax.rem(place + step, 4) for step in (1, 3, 2))
        self.messages = []

    def send(self, source, target, to):
        message = Message(self.pool, source, target, to).start()
        self.messages.append(message)
        return message

    def start_far(self):
        self.up = self.send(self.mine(self.far, 0), self.transit(0), self.plus)
        self.down = self.send(self.mine(self.far, 1), self.transit(1), self.minus)

    def start_near(self):
        self.direct_up = self.send(self.mine(self.above, 1), self.slots(0), self.plus)
        self.direct_down = self.send(self.mine(self.below, 0), self.slots(1), self.minus)

    def add(self):
        for message, half, place in ((self.up, 0, self.above), (self.down, 1, self.below)):
            message.arrived()
            piece = self.mine(place, half)
            piece[...] = (piece[...].astype(F32) + self.transit(half)[...].astype(F32)).astype(BF16)
            if half == 0:
                self.pass_up()
        self.pass_down()

    def pass_up(self):
        self.sum_up = self.send(self.mine(self.above, 0), self.slots(2), self.plus)

    def pass_down(self):
        self.sum_down = self.send(self.mine(self.below, 1), self.slots(3), self.minus)

    def arrived(self, half):
        if half == 0:
            self.direct_down.arrived()
            self.sum_up.arrived()
        else:
            self.direct_up.arrived()
            self.sum_down.arrived()

    def total(self, half):
        return (
            self.mine(self.here, half)[...].astype(F32)
            + self.slots(1 - half)[...].astype(F32)
            + self.slots(2 + half)[...].astype(F32)
        )

    def sent(self):
        for message in self.messages:
            message.sent()


def kernel(
    inputs,
    grads,
    kernel_grad,
    basis_in,
    basis_out,
    eigen_in,
    eigen_out,
    gathered,
    in_cov,
    out_cov,
    basis,
    turned,
    part,
    part_transit,
    part_slots,
    scaled,
    eigen_rows,
    eigen_columns,
    away,
    away_in,
    home,
    home_sum,
    restored_part,
    home_transit,
    home_slots,
    tokens,
    token_columns,
    grad_columns,
    grad_part,
    cov,
    cov_transit,
    cov_slots,
    cov_across,
    strips_part,
    strips,
    settled,
    swapped,
    grad_tile,
    basis_out_tile,
    local,
    send,
    receive,
):
    pool = [send, receive, 0]
    rows = kernel_grad.shape[0]
    width = kernel_grad.shape[1]
    strip = basis_in.shape[0]
    out_rows = out_cov.shape[0]
    narrow = width // 4
    dp, owner = lax.axis_index("dp"), lax.axis_index("owner")
    xh, z, c = dp // 8, lax.rem(dp // 2, 4), lax.rem(dp, 2)
    y, xl = owner // 2, lax.rem(owner, 2)
    x = xh * 2 + xl

    def device(x, y, z, c):
        x, y, z, c = lax.rem(x, 4), lax.rem(y, 4), lax.rem(z, 4), lax.rem(c, 2)
        return (x // 2) * 8 + z * 2 + c, y * 2 + lax.rem(x, 2)

    x_up, x_down, x_far = device(x + 1, y, z, c), device(x + 3, y, z, c), device(x + 2, y, z, c)
    y_up, y_down = device(x, y + 1, z, c), device(x, y + 3, z, c)
    z_up, z_down, z_far = device(x, y, z + 1, c), device(x, y, z + 3, c), device(x, y, z + 2, c)
    core = device(x, y, z, c + 1)
    pair = xh * 2 + 1 - xl
    cross = lax.rem(x + 2 * xl + 3, 4)
    plane = [(step, side) for step in (-1, 0, -2, 2) for side in (0, 1) if (step, side) != (0, 0)]
    x_pair = device(pair, y, z, c)

    locals_started = []

    def fetch(source, target):
        copy = pltpu.make_async_copy(source, target, local.at[len(locals_started)])
        copy.start()
        locals_started.append(copy)
        return copy

    def block_columns(ref, block):
        return ref.at[:, pl.ds(pl.multiple_of(block * rows, rows), rows)]

    def owner_columns(ref):
        return ref.at[:, pl.ds(pl.multiple_of(owner * width, width), width)]

    got_grad = fetch(kernel_grad, grad_tile)
    got_basis_out = fetch(basis_out, basis_out_tile)

    barrier = pltpu.get_barrier_semaphore()
    partners = [device(x + step, y, z, c + side) for step in range(4) for side in range(2) if step + side > 0]
    partners += [y_up, y_down, z_up, z_down, z_far]
    for partner in partners:
        pl.semaphore_signal(barrier, inc=1, device_id=partner, device_id_type=MESH)

    row = xh * 4 + z
    diagonal = row == owner

    def on_diagonal(row, c):
        return (row // 4) * 8 + lax.rem(row, 4) * 2 + c, owner

    mirror = [((owner // 4) * 8 + lax.rem(owner, 4) * 2 + side, row) for side in range(2)]

    @pl.when(diagonal)
    def _():
        for step in range(1, 8):
            pl.semaphore_signal(
                barrier, inc=1, device_id=on_diagonal(lax.rem(row + step, 8), c), device_id_type=MESH
            )

    @pl.when(jnp.logical_not(diagonal))
    def _():
        for to in mirror + [on_diagonal(owner, c)]:
            pl.semaphore_signal(barrier, inc=1, device_id=to, device_id_type=MESH)


    def strip_rows(x, y, c):
        block = (x // 2) * 2 + c
        start = pl.multiple_of((y * 2 + lax.rem(x, 2)) * strip, strip)
        return block, pl.ds(start, strip)

    my_block, my_rows = strip_rows(x, y, c)

    def basis_piece(t):
        return basis.at[my_block, my_rows, t * rows : (t + 1) * rows]

    own_basis = [
        fetch(block_columns(basis_in, xh * 8 + (2 * xl + t) * 2 + c), basis_piece(t)) for t in range(2)
    ]
    far, above, below = lax.rem(z + 2, 4), lax.rem(z + 1, 4), lax.rem(z + 3, 4)
    order = [far, above, below, z]
    got_tokens = {}
    got_columns = fetch(owner_columns(inputs), token_columns.at[0])
    got_grad_columns = fetch(owner_columns(grads), grad_columns.at[0])
    for step in range(4):
        for high in range(2):
            got_tokens[step, high] = fetch(
                block_columns(inputs, high * 8 + order[step] * 2 + c), tokens.at[0, step * 2 + high]
            )

    pl.semaphore_wait(barrier, len(partners) + jnp.where(diagonal, 7, 3))

    scatter_basis = {}
    for step, side in plane:
        to = {-1: pair, -2: cross, 0: x, 2: lax.rem(x + 2, 4)}[step]
        to_c = lax.rem(c + side, 2)
        for t in range(2):
            block = (to // 2) * 8 + (2 * lax.rem(to, 2) + t) * 2 + to_c
            scatter_basis[step, side, t] = Message(
                pool, block_columns(basis_in, block), basis_piece(t), device(to, y, z, to_c)
            ).start()
    small = []
    eigen_rows[z] = jnp.broadcast_to(eigen_in[...].reshape(1, rows), (8, rows))
    eigen_columns[xl] = jnp.broadcast_to(eigen_out[...].reshape(1, width), (8, width))
    for to in (z_up, z_down, z_far):
        small.append(Message(pool, eigen_rows.at[z], eigen_rows.at[z], to).start())
    small.append(Message(pool, eigen_columns.at[xl], eigen_columns.at[xl], x_pair).start())

    token_messages = {}
    column_message = Message(pool, owner_columns(inputs), token_columns.at[1], core).start()
    for step in range(4):
        for high in range(2):
            token_messages[step, high] = Message(
                pool,
                block_columns(inputs, high * 8 + order[step] * 2 + 1 - c),
                tokens.at[1, step * 2 + high],
                core,
            ).start()
    grad_message = Message(pool, owner_columns(grads), grad_columns.at[1], core).start()

    got_grad.wait()
    got_basis_out.wait()

    def turned_tile(x, c):
        return turned.at[lax.rem(x, 2), (x // 2) * 2 + c]

    turned_tile(x, c)[...] = dot(grad_tile[...], basis_out_tile[...]).astype(BF16)
    half_rows = rows // 2

    def turned_region(place, half):
        return turned.at[lax.rem(place, 2), (place // 2) * 2 + c, half * half_rows : (half + 1) * half_rows]

    def to_core(step):
        tile = turned_tile(lax.rem(x + step, 4), c)
        return Message(pool, tile, tile, core).start()

    turned_gather = Gather(pool, turned_region, x, x_up, x_down)

    def basis_region(place, half):
        start = pl.multiple_of(place * 2 * strip, 2 * strip)
        high = 2 * lax.rem(xh + half, 2)
        return basis.at[pl.ds(high, 2), pl.ds(start, 2 * strip), :]

    basis_gather = Gather(pool, basis_region, y, y_up, y_down)
    for copy in own_basis:
        copy.wait()
    for (step, side, t), message in scatter_basis.items():
        if step in (-1, 0):
            message.arrived()
    basis_gather.start(0)
    turned_gather.start(0)
    for (step, side, t), message in scatter_basis.items():
        if step not in (-1, 0):
            message.arrived()
    basis_gather.start(1)
    turned_gather.start(1)
    turned_core = [to_core(0)]

    def cov_mine(place, half):
        return cov.at[half, place]

    cov_scatter = Scatter(
        pool, cov_mine, lambda half: cov_transit.at[half], lambda slot: cov_slots.at[slot], z, z_up, z_down
    )
    got_columns.wait()
    got_grad_columns.wait()
    column_message.arrived()
    grad_message.arrived()
    grad_part[...] = (
        dot_rows(grad_columns[0], grad_columns[0]) + dot_rows(grad_columns[1], grad_columns[1])
    ).astype(BF16)

    def half_columns(number, side):
        return token_columns[number, :, pl.ds(pl.multiple_of(side * rows, rows), rows)]

    strips_part[...] = (
        dot_rows(half_columns(0, c), half_columns(0, 1 - c)) + dot_rows(half_columns(1, c), half_columns(1, 1 - c))
    ).astype(BF16)

    def own_side(row):
        return jnp.where(row <= owner, c, 1 - c)

    def cov_product(step):
        for high in range(2):
            got_tokens[step, high].wait()
            token_messages[step, high].arrived()
        place = order[step]

        def product(high, unused):
            side = own_side(high * 4 + place)
            tile = dot_rows(tokens[0, step * 2 + high], half_columns(0, side))
            tile = tile + dot_rows(tokens[1, step * 2 + high], half_columns(1, side))
            cov[high, place, :rows] = tile.astype(BF16)
            start = pl.multiple_of((high * 8 + place * 2 + c) * out_rows, out_rows)
            cov[high, place, rows : rows + out_rows] = grad_part[pl.ds(start, out_rows), :rows]
            cov[high, place, rows + out_rows : rows + 2 * out_rows] = grad_part[pl.ds(start, out_rows), rows:]
            start = pl.multiple_of((high * 4 + place) * out_rows, out_rows)
            cov[high, place, rows + 2 * out_rows :] = strips_part[pl.ds(start, out_rows), :]
            return unused

        lax.fori_loop(0, 2, product, 0)

    cov_product(0)
    cov_scatter.start_far()
    turned_gather.forward()
    turned_gather.near()
    turned_core += [to_core(1), to_core(3)]
    basis_gather.forward()
    cov_product(1)
    cov_product(2)
    cov_scatter.start_near()
    cov_product(3)
    cov_scatter.add()
    turned_gather.far()
    turned_core.append(to_core(2))
    basis_gather.near()
    basis_gather.far()
    for message in turned_core:
        message.arrived()

    wave = width // WAVES

    def rows_of(ref, place, half, number):
        start = pl.multiple_of(place * narrow, narrow)
        return ref.at[half, pl.ds(start, narrow), number * wave : (number + 1) * wave]

    part_scatters = [
        Scatter(
            pool,
            lambda place, half, number=number: rows_of(part, place, half, number),
            lambda half, number=number: part_transit.at[number, half],
            lambda slot, number=number: part_slots.at[number, slot],
            z,
            z_up,
            z_down,
        )
        for number in range(WAVES)
    ]

    def rotate(t, number):
        start = pl.multiple_of(t * rows, rows)
        left = basis[:, :, pl.ds(start, rows)].reshape(4 * rows, rows)

        def one(side, unused):
            right = turned[side, :, :, number * wave : (number + 1) * wave].reshape(4 * rows, wave)
            part[side, pl.ds(start, rows), number * wave : (number + 1) * wave] = dot_rows(left, right).astype(BF16)
            return unused

        lax.fori_loop(0, 2, one, 0)

    for number, scatter in enumerate(part_scatters):
        rotate(1 - z // 2, number)
        scatter.start_far()
        if number > 0:
            part_scatters[number - 1].add()
        rotate(z // 2, number)
        scatter.start_near()

    cov_scatter.arrived(0)
    cov_scatter.arrived(1)
    cov[1 - xh, z] = cov_scatter.total(1 - xh).astype(BF16)
    cov_message = Message(pool, cov.at[1 - xh, z], cov_across, x_far).start()

    for message in small:
        message.arrived()
    line = eigen_rows[2 * xl + z // 2]
    line = jnp.where(lax.rem(z, 2) == 0, line[:, :narrow], line[:, narrow:])
    column = jnp.transpose(jnp.broadcast_to(line[:1], (128, narrow)))[:, :1]

    scaled_gathers = []
    for number, scatter in enumerate(part_scatters):
        gather = Gather(
            pool, lambda place, half, number=number: rows_of(scaled, place, half, number), z, z_up, z_down
        )
        for half in range(2):
            scatter.arrived(half)
            divisor = column * eigen_columns[half, :1, number * wave : (number + 1) * wave] + damping
            rows_of(scaled, z, half, number)[...] = (scatter.total(half) / divisor).astype(BF16)
            gather.start(half)
        scaled_gathers.append(gather)
        if number + 1 < WAVES:
            if number + 2 == WAVES:
                part_scatters[number + 1].add()
            gather.forward()

    cov_message.arrived()
    total = cov_scatter.total(xh) + cov_across[...].astype(F32)
    settled[...] = total.astype(BF16)
    out_cov[:, :rows] = total[rows : rows + out_rows]
    out_cov[:, rows:] = total[rows + out_rows : rows + 2 * out_rows]
    side = own_side(row)
    own_half = pl.ds(pl.multiple_of(side * rows, rows), rows)
    other_half = pl.ds(pl.multiple_of((1 - side) * rows, rows), rows)
    in_cov[:, own_half] = total[:rows]
    my_strip = pl.ds(pl.multiple_of(row * out_rows, out_rows), out_rows)
    mirror_core = jnp.where(row < owner, c, 1 - c)
    swap = Message(pool, settled.at[:rows], swapped, (mirror[0][0] + mirror_core, row))
    strip_message = Message(
        pool, settled.at[rows + 2 * out_rows :], strips.at[my_strip, :], on_diagonal(owner, c)
    )
    seven_wait = pltpu.make_async_remote_copy(
        src_ref=strips.at[: 7 * out_rows],
        dst_ref=strips.at[: 7 * out_rows],
        send_sem=strip_message.sems[0],
        recv_sem=strip_message.sems[1],
        device_id=on_diagonal(owner, c),
        device_id_type=MESH,
    )

    @pl.when(jnp.logical_not(diagonal))
    def _():
        swap.start()
        strip_message.start()

    lines = rows // CHUNKS
    half_lines = lines // 2
    crossings, sums, ends, to_core_last = [], [], [], []

    def pass_to_core(ref):
        to_core_last.append(Message(pool, ref, ref, core).start())

    def start_sum(number):
        def partial(side, target):
            def one(place, unused):
                left = basis[(place // 2) * 2 + side]
                right = scaled[lax.rem(place, 2), :, number * wave : (number + 1) * wave]
                target[place] = dot(left, right).astype(target.dtype)
                return unused

            lax.fori_loop(0, 4, one, 0)

        partial(1 - c, away.at[number])
        crossings.append(Message(pool, away.at[number], away_in.at[number], core).start())
        partial(c, home)

    def cross_sum(number, count):
        crossings[number].arrived()
        home_sum[number] = (home[...] + away_in[number].astype(F32)).astype(BF16)
        size = rows // count // 2
        for chunk in range(count):
            sums.append(
                Scatter(
                    pool,
                    lambda place, half, start=chunk * 2 * size: home_sum.at[
                        number, place, start + half * size : start + (half + 1) * size, :
                    ],
                    lambda half, start=chunk * size: home_transit.at[number, half, start : start + size, :],
                    lambda slot, start=chunk * size: home_slots.at[number, slot, start : start + size, :],
                    x,
                    x_up,
                    x_down,
                )
            )

    def finish_sum(scatter):
        scatter.arrived(0)
        scatter.arrived(1)
        return jnp.concatenate([scatter.total(0), scatter.total(1)], axis=0).astype(BF16)

    for number, gather in enumerate(scaled_gathers):
        gather.near()
        gather.far()
        start_sum(number)
        if number + 1 < WAVES:
            scaled_gathers[number + 1].forward()
            cross_sum(number, 1)
            sums[number].start_far()
            sums[number].start_near()
        else:
            for before in sums:
                before.add()
            cross_sum(number, CHUNKS)
    last_sums = sums[WAVES - 1 :]
    last_sums[0].start_far()
    last_sums[0].start_near()
    if CHUNKS > 1:
        last_sums[1].start_far()
    for number in range(WAVES - 1):
        restored_part[:, number * wave : (number + 1) * wave] = finish_sum(sums[number])

    def finish_chunk(chunk):
        chunk_rows = slice(chunk * lines, (chunk + 1) * lines)
        restored_part[chunk_rows, (WAVES - 1) * wave :] = finish_sum(last_sums[chunk])
        new = lax.dot_general(
            restored_part[chunk_rows, :],
            basis_out_tile[...],
            (((1,), (1,)), ((), ())),
            preferred_element_type=F32,
        )

        def region(place, half, high):
            start = (high * 8 + place * 2 + c) * rows + chunk * lines
            if half is None:
                return gathered.at[pl.ds(pl.multiple_of(start, 16), lines), :]
            return gathered.at[pl.ds(pl.multiple_of(start + half * half_lines, 16), half_lines), :]

        own = Gather(pool, functools.partial(region, high=xh), z, z_up, z_down)
        other = Gather(pool, functools.partial(region, high=1 - xh), z, z_up, z_down)
        mine = region(z, None, xh)
        mine[...] = new.astype(BF16)
        across = Message(pool, mine, mine, x_far).start()
        own.start(0)
        own.start(1)
        pass_to_core(mine)
        ends.append((own, other, across, region))

    def start_other(chunk):
        own, other, across, region = ends[chunk]
        across.arrived()
        other.start(0)
        other.start(1)
        pass_to_core(region(z, None, 1 - xh))

    def forward(chunk, high):
        gather = ends[chunk][high]
        region = ends[chunk][3]
        gather.forward()
        gather.near()
        for place in (above, below):
            pass_to_core(region(place, None, xh if high == 0 else 1 - xh))

    def last(chunk, high):
        ends[chunk][high].far()
        pass_to_core(ends[chunk][3](far, None, xh if high == 0 else 1 - xh))

    last_sums[0].add()
    for chunk in range(CHUNKS):
        if chunk + 1 < CHUNKS:
            last_sums[chunk + 1].start_near()
        if chunk + 2 < CHUNKS:
            last_sums[chunk + 2].start_far()
        finish_chunk(chunk)
        if chunk + 1 < CHUNKS:
            last_sums[chunk + 1].add()
        if chunk >= 1:
            forward(chunk - 1, 0)
            start_other(chunk - 1)
        if chunk >= 2:
            forward(chunk - 2, 1)
    forward(CHUNKS - 1, 0)
    start_other(CHUNKS - 1)
    if CHUNKS > 1:
        forward(CHUNKS - 2, 1)

    forward(CHUNKS - 1, 1)
    for chunk in range(CHUNKS):
        last(chunk, 0)

    @pl.when(diagonal)
    def _():
        strips[my_strip, :] = settled[rows + 2 * out_rows :]
        seven_wait.wait_recv()
        in_cov[:, other_half] = strips[...].astype(F32)

    @pl.when(jnp.logical_not(diagonal))
    def _():
        swap.arrived()
        in_cov[:, other_half] = jnp.transpose(swapped[...].astype(F32))
        swap.sent()
        strip_message.sent()

    for chunk in range(CHUNKS):
        last(chunk, 1)

    for message in to_core_last:
        message.arrived()
    for own, other, across, region in ends:
        own.sent()
        other.sent()
        across.sent()
    for message in crossings + to_core_last + list(scatter_basis.values()) + small + turned_core:
        message.sent()
    for message in list(token_messages.values()) + [column_message, grad_message, cov_message]:
        message.sent()
    for group in [turned_gather, basis_gather, cov_scatter] + part_scatters + scaled_gathers + sums:
        group.sent()


def finish(gathered, in_cov, out_cov, old_in, old_out, precond, in_factor, out_factor, new_in, new_out, sem, tokens):
    copies = [pltpu.make_async_copy(gathered, precond, sem.at[0])]
    copies[0].start()
    new_in[...] = factor_decay * old_in[...] + (1.0 - factor_decay) * in_cov[...] / tokens
    new_out[...] = factor_decay * old_out[...] + (1.0 - factor_decay) * out_cov[...] / tokens
    copies += [pltpu.make_async_copy(new_in, in_factor, sem.at[1])]
    copies += [pltpu.make_async_copy(new_out, out_factor, sem.at[2])]
    for copy in copies[1:]:
        copy.start()
    for copy in copies:
        copy.wait()


def shards(
    inputs, out_grads, kernel_grad, basis_in, basis_out, eigen_in, eigen_out, old_in_factor, old_out_factor
):
    rows, width = kernel_grad.shape
    strip = basis_in.shape[0]
    tokens = inputs.shape[0]
    out_rows = old_out_factor.shape[0]
    deep = rows + 3 * out_rows
    total = 16 * rows
    narrow = width // 4
    anywhere = pl.BlockSpec(memory_space=pl.ANY)
    vmem = pl.BlockSpec(memory_space=pltpu.VMEM)
    scratch = [
        pltpu.VMEM((4, rows, 2 * rows), BF16),
        pltpu.VMEM((2, 4, rows, width), BF16),
        pltpu.VMEM((2, 4 * narrow, width), BF16),
        pltpu.VMEM((WAVES, 2, narrow, width // WAVES), BF16),
        pltpu.VMEM((WAVES, 4, narrow, width // WAVES), BF16),
        pltpu.VMEM((2, 4 * narrow, width), BF16),
        pltpu.VMEM((4, 8, rows), F32),
        pltpu.VMEM((2, 8, width), F32),
        pltpu.VMEM((WAVES, 4, rows, width // WAVES), BF16),
        pltpu.VMEM((WAVES, 4, rows, width // WAVES), BF16),
        pltpu.VMEM((4, rows, width // WAVES), F32),
        pltpu.VMEM((WAVES, 4, rows, width // WAVES), BF16),
        pltpu.VMEM((rows, width), BF16),
        pltpu.VMEM((WAVES, 2, rows // 2, width // WAVES), BF16),
        pltpu.VMEM((WAVES, 4, rows // 2, width // WAVES), BF16),
        pltpu.VMEM((2, 8, tokens, rows), BF16),
        pltpu.VMEM((2, tokens, width), BF16),
        pltpu.VMEM((2, tokens, width), BF16),
        pltpu.VMEM((width, width), BF16),
        pltpu.VMEM((2, 4, deep, rows), BF16),
        pltpu.VMEM((2, deep, rows), BF16),
        pltpu.VMEM((4, deep, rows), BF16),
        pltpu.VMEM((deep, rows), BF16),
        pltpu.VMEM((rows, rows), BF16),
        pltpu.VMEM((rows, rows), BF16),
        pltpu.VMEM((deep, rows), BF16),
        pltpu.VMEM((rows, rows), BF16),
        pltpu.VMEM((rows, width), BF16),
        pltpu.VMEM((width, width), BF16),
        pltpu.SemaphoreType.DMA((16,)),
        pltpu.SemaphoreType.DMA((MESSAGES,)),
        pltpu.SemaphoreType.DMA((MESSAGES,)),
    ]
    gathered, in_cov, out_cov = pl.pallas_call(
        kernel,
        out_shape=(
            pltpu.VMEM((total, width), BF16),
            pltpu.VMEM((rows, width), F32),
            pltpu.VMEM((out_rows, width), F32),
        ),
        in_specs=[anywhere] * 5 + [vmem] * 2,
        out_specs=(vmem, vmem, vmem),
        scratch_shapes=scratch,
        compiler_params=pltpu.CompilerParams(
            collective_id=0, has_side_effects=True, vmem_limit_bytes=52 * 2**20
        ),
        cost_estimate=pl.CostEstimate(flops=2 * 10**10, bytes_accessed=4 * 10**7, transcendentals=0),
        name="precondition",
    )(
        inputs,
        out_grads,
        kernel_grad,
        basis_in,
        basis_out,
        eigen_in,
        eigen_out,
    )
    return pl.pallas_call(
        functools.partial(finish, tokens=16 * tokens),
        out_shape=(
            jax.ShapeDtypeStruct((total, width), BF16),
            jax.ShapeDtypeStruct((rows, width), F32),
            jax.ShapeDtypeStruct((out_rows, width), F32),
        ),
        in_specs=[vmem] * 5,
        out_specs=(anywhere, anywhere, anywhere),
        scratch_shapes=[pltpu.VMEM((rows, width), F32), pltpu.VMEM((out_rows, width), F32), pltpu.SemaphoreType.DMA((3,))],
        compiler_params=pltpu.CompilerParams(vmem_limit_bytes=40 * 2**20),
        name="finish",
    )(gathered, in_cov, out_cov, old_in_factor, old_out_factor)


def solution(mesh):
    in_specs = (
        P("dp", None),
        P("dp", None),
        P("dp", "owner"),
        P(("dp", "owner"), None),
        P("owner", None),
        P("dp"),
        P("owner"),
        P("dp", "owner"),
        P(("owner", "dp"), None),
    )
    out_specs = (P(None, "owner"), P("dp", "owner"), P(("owner", "dp"), None))
    return jax.shard_map(shards, mesh=mesh, in_specs=in_specs, out_specs=out_specs, check_vma=False)
```

```python
import functools

import jax
import jax.numpy as jnp
from jax import lax
from jax.experimental import pallas as pl
from jax.experimental.pallas import tpu as pltpu
from jax.sharding import PartitionSpec as P

damping = 0.3
factor_decay = 0.9
MESH = pl.DeviceIdType.MESH
CHUNKS = 3
WAVES = 2
MESSAGES = 256
F32 = jnp.float32
BF16 = jnp.bfloat16


def dot_rows(left, right):
    return lax.dot_general(left, right, (((0,), (0,)), ((), ())), preferred_element_type=F32)


def dot(left, right):
    return jnp.dot(left, right, preferred_element_type=F32)


class Message:
    def __init__(self, pool, source, target, to):
        number = pool[2]
        pool[2] += 1
        self.copy = pltpu.make_async_remote_copy(
            src_ref=source,
            dst_ref=target,
            send_sem=pool[0].at[number],
            recv_sem=pool[1].at[number],
            device_id=to,
            device_id_type=MESH,
        )

    def start(self):
        self.copy.start()
        return self

    def arrived(self):
        self.copy.wait_recv()

    def sent(self):
        self.copy.wait_send()


class Gather:
    def __init__(self, pool, region, place, plus, minus):
        self.region, self.place, self.plus, self.minus, self.pool = region, place, plus, minus, pool
        self.own = {}
        self.passed = []

    def message(self, shard, half, to):
        piece = self.region(shard, half)
        return Message(self.pool, piece, piece, to).start()

    def start(self, half):
        order = (("plus", self.plus), ("minus", self.minus))
        for name, to in order if half == 0 else order[::-1]:
            self.own[name, half] = self.message(self.place, half, to)

    def forward(self):
        below, above = lax.rem(self.place + 3, 4), lax.rem(self.place + 1, 4)
        self.own["plus", 0].arrived()
        self.passed.append(self.message(below, 0, self.plus))
        self.own["minus", 1].arrived()
        self.passed.append(self.message(above, 1, self.minus))

    def near(self):
        self.own["minus", 0].arrived()
        self.own["plus", 1].arrived()

    def far(self):
        for message in self.passed:
            message.arrived()

    def sent(self):
        for message in list(self.own.values()) + self.passed:
            message.sent()


class Scatter:
    def __init__(self, pool, mine, transit, slots, place, plus, minus):
        self.pool, self.mine, self.transit, self.slots = pool, mine, transit, slots
        self.plus, self.minus = plus, minus
        self.here = place
        self.above, self.below, self.far = (lax.rem(place + step, 4) for step in (1, 3, 2))
        self.messages = []

    def send(self, source, target, to):
        message = Message(self.pool, source, target, to).start()
        self.messages.append(message)
        return message

    def start_far(self):
        self.up = self.send(self.mine(self.far, 0), self.transit(0), self.plus)
        self.down = self.send(self.mine(self.far, 1), self.transit(1), self.minus)

    def start_near(self):
        self.direct_up = self.send(self.mine(self.above, 1), self.slots(0), self.plus)
        self.direct_down = self.send(self.mine(self.below, 0), self.slots(1), self.minus)

    def add(self):
        for message, half, place in ((self.up, 0, self.above), (self.down, 1, self.below)):
            message.arrived()
            piece = self.mine(place, half)
            piece[...] = (piece[...].astype(F32) + self.transit(half)[...].astype(F32)).astype(BF16)
            if half == 0:
                self.pass_up()
        self.pass_down()

    def pass_up(self):
        self.sum_up = self.send(self.mine(self.above, 0), self.slots(2), self.plus)

    def pass_down(self):
        self.sum_down = self.send(self.mine(self.below, 1), self.slots(3), self.minus)

    def arrived(self, half):
        if half == 0:
            self.direct_down.arrived()
            self.sum_up.arrived()
        else:
            self.direct_up.arrived()
            self.sum_down.arrived()

    def total(self, half):
        return (
            self.mine(self.here, half)[...].astype(F32)
            + self.slots(1 - half)[...].astype(F32)
            + self.slots(2 + half)[...].astype(F32)
        )

    def sent(self):
        for message in self.messages:
            message.sent()


def kernel(
    inputs,
    grads,
    kernel_grad,
    basis_in,
    basis_out,
    eigen_in,
    eigen_out,
    gathered,
    in_cov,
    out_cov,
    basis,
    turned,
    part,
    part_transit,
    part_slots,
    scaled,
    eigen_rows,
    eigen_columns,
    away,
    away_in,
    home,
    home_sum,
    restored_part,
    home_transit,
    home_slots,
    tokens,
    token_columns,
    grad_columns,
    grad_part,
    cov,
    cov_transit,
    cov_slots,
    cov_across,
    right,
    right_in,
    right_transit,
    right_slots,
    grad_tile,
    basis_out_tile,
    local,
    send,
    receive,
):
    pool = [send, receive, 0]
    rows = kernel_grad.shape[0]
    width = kernel_grad.shape[1]
    strip = basis_in.shape[0]
    out_rows = out_cov.shape[0]
    narrow = width // 4
    dp, owner = lax.axis_index("dp"), lax.axis_index("owner")
    xh, z, c = dp // 8, lax.rem(dp // 2, 4), lax.rem(dp, 2)
    y, xl = owner // 2, lax.rem(owner, 2)
    x = xh * 2 + xl

    def device(x, y, z, c):
        x, y, z, c = lax.rem(x, 4), lax.rem(y, 4), lax.rem(z, 4), lax.rem(c, 2)
        return (x // 2) * 8 + z * 2 + c, y * 2 + lax.rem(x, 2)

    x_up, x_down, x_far = device(x + 1, y, z, c), device(x + 3, y, z, c), device(x + 2, y, z, c)
    y_up, y_down = device(x, y + 1, z, c), device(x, y + 3, z, c)
    z_up, z_down, z_far = device(x, y, z + 1, c), device(x, y, z + 3, c), device(x, y, z + 2, c)
    core = device(x, y, z, c + 1)
    pair = xh * 2 + 1 - xl
    cross = lax.rem(x + 2 * xl + 3, 4)
    plane = [(step, side) for step in (-1, 0, -2, 2) for side in (0, 1) if (step, side) != (0, 0)]
    x_pair = device(pair, y, z, c)

    locals_started = []

    def fetch(source, target):
        copy = pltpu.make_async_copy(source, target, local.at[len(locals_started)])
        copy.start()
        locals_started.append(copy)
        return copy

    def block_columns(ref, block):
        return ref.at[:, pl.ds(pl.multiple_of(block * rows, rows), rows)]

    def owner_columns(ref):
        return ref.at[:, pl.ds(pl.multiple_of(owner * width, width), width)]

    got_grad = fetch(kernel_grad, grad_tile)
    got_basis_out = fetch(basis_out, basis_out_tile)

    barrier = pltpu.get_barrier_semaphore()
    partners = [device(x + step, y, z, c + side) for step in range(4) for side in range(2) if step + side > 0]
    partners += [y_up, y_down, z_up, z_down, z_far]
    for partner in partners:
        pl.semaphore_signal(barrier, inc=1, device_id=partner, device_id_type=MESH)

    def strip_rows(x, y, c):
        block = (x // 2) * 2 + c
        start = pl.multiple_of((y * 2 + lax.rem(x, 2)) * strip, strip)
        return block, pl.ds(start, strip)

    my_block, my_rows = strip_rows(x, y, c)

    def basis_piece(t):
        return basis.at[my_block, my_rows, t * rows : (t + 1) * rows]

    own_basis = [
        fetch(block_columns(basis_in, xh * 8 + (2 * xl + t) * 2 + c), basis_piece(t)) for t in range(2)
    ]
    far, above, below = lax.rem(z + 2, 4), lax.rem(z + 1, 4), lax.rem(z + 3, 4)
    order = [far, above, below, z]
    got_tokens = {}
    got_columns = fetch(owner_columns(inputs), token_columns.at[0])
    got_grad_columns = fetch(owner_columns(grads), grad_columns.at[0])
    for step in range(4):
        for high in range(2):
            got_tokens[step, high] = fetch(
                block_columns(inputs, high * 8 + order[step] * 2 + c), tokens.at[0, step * 2 + high]
            )

    pl.semaphore_wait(barrier, len(partners))

    scatter_basis = {}
    for step, side in plane:
        to = {-1: pair, -2: cross, 0: x, 2: lax.rem(x + 2, 4)}[step]
        to_c = lax.rem(c + side, 2)
        for t in range(2):
            block = (to // 2) * 8 + (2 * lax.rem(to, 2) + t) * 2 + to_c
            scatter_basis[step, side, t] = Message(
                pool, block_columns(basis_in, block), basis_piece(t), device(to, y, z, to_c)
            ).start()
    small = []
    eigen_rows[z] = jnp.broadcast_to(eigen_in[...].reshape(1, rows), (8, rows))
    eigen_columns[xl] = jnp.broadcast_to(eigen_out[...].reshape(1, width), (8, width))
    for to in (z_up, z_down, z_far):
        small.append(Message(pool, eigen_rows.at[z], eigen_rows.at[z], to).start())
    small.append(Message(pool, eigen_columns.at[xl], eigen_columns.at[xl], x_pair).start())

    token_messages = {}
    column_message = Message(pool, owner_columns(inputs), token_columns.at[1], core).start()
    grad_message = Message(pool, owner_columns(grads), grad_columns.at[1], core).start()
    for step in range(4):
        for high in range(2):
            token_messages[step, high] = Message(
                pool,
                block_columns(inputs, high * 8 + order[step] * 2 + 1 - c),
                tokens.at[1, step * 2 + high],
                core,
            ).start()

    got_grad.wait()
    got_basis_out.wait()

    def turned_tile(x, c):
        return turned.at[lax.rem(x, 2), (x // 2) * 2 + c]

    turned_tile(x, c)[...] = dot(grad_tile[...], basis_out_tile[...]).astype(BF16)
    half_rows = rows // 2

    def turned_region(place, half):
        return turned.at[lax.rem(place, 2), (place // 2) * 2 + c, half * half_rows : (half + 1) * half_rows]

    def to_core(step):
        tile = turned_tile(lax.rem(x + step, 4), c)
        return Message(pool, tile, tile, core).start()

    turned_gather = Gather(pool, turned_region, x, x_up, x_down)

    def basis_region(place, half):
        start = pl.multiple_of(place * 2 * strip, 2 * strip)
        high = 2 * lax.rem(xh + half, 2)
        return basis.at[pl.ds(high, 2), pl.ds(start, 2 * strip), :]

    basis_gather = Gather(pool, basis_region, y, y_up, y_down)
    for copy in own_basis:
        copy.wait()
    for (step, side, t), message in scatter_basis.items():
        if step in (-1, 0):
            message.arrived()
    basis_gather.start(0)
    turned_gather.start(0)
    def cov_mine(place, half):
        return cov.at[half, place]

    cov_scatter = Scatter(
        pool, cov_mine, lambda half: cov_transit.at[half], lambda slot: cov_slots.at[slot], z, z_up, z_down
    )
    half_rows = rows // 2

    def right_mine(place, half):
        return right.at[xh, place, half * half_rows : (half + 1) * half_rows, :]

    right_scatter = Scatter(
        pool, right_mine, lambda half: right_transit.at[half], lambda slot: right_slots.at[slot], z, z_up, z_down
    )
    got_columns.wait()
    got_grad_columns.wait()
    column_message.arrived()
    grad_message.arrived()
    grad_part[...] = (
        dot_rows(grad_columns[0], grad_columns[0]) + dot_rows(grad_columns[1], grad_columns[1])
    ).astype(BF16)

    def cov_product(step):
        for high in range(2):
            got_tokens[step, high].wait()
            token_messages[step, high].arrived()
        place = order[step]

        def product(high, unused):
            tile = dot_rows(tokens[0, step * 2 + high], token_columns[0])
            tile = tile + dot_rows(tokens[1, step * 2 + high], token_columns[1])
            cov[high, place, :rows] = tile[:, :rows].astype(BF16)
            right[high, place] = tile[:, rows:].astype(BF16)
            start = pl.multiple_of((high * 8 + place * 2 + c) * out_rows, out_rows)
            cov[high, place, rows : rows + out_rows] = grad_part[pl.ds(start, out_rows), :rows]
            cov[high, place, rows + out_rows :] = grad_part[pl.ds(start, out_rows), rows:]
            return unused

        lax.fori_loop(0, 2, product, 0)

    cov_product(0)
    cov_scatter.start_far()
    for (step, side, t), message in scatter_basis.items():
        if step not in (-1, 0):
            message.arrived()
    basis_gather.start(1)
    turned_gather.start(1)
    turned_core = [to_core(0)]
    cov_product(1)
    cov_product(2)
    cov_scatter.start_near()
    turned_gather.forward()
    basis_gather.forward()
    cov_product(3)
    turned_gather.near()
    turned_core += [to_core(1), to_core(3)]
    right_message = Message(pool, right.at[1 - xh], right_in, x_far).start()
    cov_scatter.add()
    turned_gather.far()
    turned_core.append(to_core(2))
    basis_gather.near()
    basis_gather.far()
    for message in turned_core:
        message.arrived()

    wave = width // WAVES

    def rows_of(ref, place, half, number):
        start = pl.multiple_of(place * narrow, narrow)
        return ref.at[half, pl.ds(start, narrow), number * wave : (number + 1) * wave]

    part_scatters = [
        Scatter(
            pool,
            lambda place, half, number=number: rows_of(part, place, half, number),
            lambda half, number=number: part_transit.at[number, half],
            lambda slot, number=number: part_slots.at[number, slot],
            z,
            z_up,
            z_down,
        )
        for number in range(WAVES)
    ]

    def rotate(t, number):
        start = pl.multiple_of(t * rows, rows)
        left = basis[:, :, pl.ds(start, rows)].reshape(4 * rows, rows)

        def one(side, unused):
            right = turned[side, :, :, number * wave : (number + 1) * wave].reshape(4 * rows, wave)
            part[side, pl.ds(start, rows), number * wave : (number + 1) * wave] = dot_rows(left, right).astype(BF16)
            return unused

        lax.fori_loop(0, 2, one, 0)

    for number, scatter in enumerate(part_scatters):
        rotate(1 - z // 2, number)
        scatter.start_far()
        if number > 0:
            part_scatters[number - 1].add()
        rotate(z // 2, number)
        scatter.start_near()

    cov_scatter.arrived(0)
    cov_scatter.arrived(1)
    cov[1 - xh, z] = cov_scatter.total(1 - xh).astype(BF16)
    cov_message = Message(pool, cov.at[1 - xh, z], cov_across, x_far).start()

    for message in small:
        message.arrived()
    line = eigen_rows[2 * xl + z // 2]
    line = jnp.where(lax.rem(z, 2) == 0, line[:, :narrow], line[:, narrow:])
    column = jnp.transpose(jnp.broadcast_to(line[:1], (128, narrow)))[:, :1]

    scaled_gathers = []
    for number, scatter in enumerate(part_scatters):
        gather = Gather(
            pool, lambda place, half, number=number: rows_of(scaled, place, half, number), z, z_up, z_down
        )
        for half in range(2):
            scatter.arrived(half)
            divisor = column * eigen_columns[half, :1, number * wave : (number + 1) * wave] + damping
            rows_of(scaled, z, half, number)[...] = (scatter.total(half) / divisor).astype(BF16)
            gather.start(half)
        scaled_gathers.append(gather)
        if number + 1 < WAVES:
            if number + 2 == WAVES:
                part_scatters[number + 1].add()
            gather.forward()

    lines = rows // CHUNKS
    half_lines = lines // 2
    crossings, sums, ends, to_core_last = [], [], [], []

    def pass_to_core(ref):
        to_core_last.append(Message(pool, ref, ref, core).start())

    def start_sum(number, start, size):
        chunk_rows = slice(start, start + size)

        def partial(side, target):
            def one(place, unused):
                left = basis[(place // 2) * 2 + side, chunk_rows, :]
                right = scaled[lax.rem(place, 2), :, number * wave : (number + 1) * wave]
                target[place, chunk_rows, :] = dot(left, right).astype(target.dtype)
                return unused

            lax.fori_loop(0, 4, one, 0)

        partial(1 - c, away.at[number])
        crossing = Message(
            pool, away.at[number, :, chunk_rows, :], away_in.at[number, :, chunk_rows, :], core
        ).start()
        crossings.append(crossing)
        partial(c, home)

        def cross():
            crossing.arrived()
            home_sum[number, :, chunk_rows, :] = (
                home[:, chunk_rows, :] + away_in[number, :, chunk_rows, :].astype(F32)
            ).astype(BF16)
            half = size // 2
            scatter = Scatter(
                pool,
                lambda place, part_of: home_sum.at[
                    number, place, start + part_of * half : start + (part_of + 1) * half, :
                ],
                lambda part_of: home_transit.at[number, part_of, start // 2 : start // 2 + half, :],
                lambda slot: home_slots.at[number, slot, start // 2 : start // 2 + half, :],
                x,
                x_up,
                x_down,
            )
            scatter.start_far()
            scatter.start_near()
            sums.append(scatter)

        return cross

    def finish_sum(scatter):
        scatter.arrived(0)
        scatter.arrived(1)
        return jnp.concatenate([scatter.total(0), scatter.total(1)], axis=0).astype(BF16)

    right_message.arrived()
    right[xh] = (right[xh].astype(F32) + right_in[...].astype(F32)).astype(BF16)

    scaled_gathers[0].near()
    scaled_gathers[0].far()
    cross = start_sum(0, 0, rows)
    scaled_gathers[1].forward()
    cross()
    right_scatter.start_far()
    right_scatter.start_near()
    sums[0].add()
    scaled_gathers[1].near()
    scaled_gathers[1].far()
    crosses = [start_sum(1, 0, lines)]
    for chunk in range(CHUNKS):
        if chunk + 1 < CHUNKS:
            crosses.append(start_sum(1, (chunk + 1) * lines, lines))
        crosses[chunk]()
        if chunk == 1:
            right_scatter.add()
            sums[1].add()
    restored_part[:, :wave] = finish_sum(sums[0])
    last_sums = sums[1:]

    def finish_chunk(chunk):
        chunk_rows = slice(chunk * lines, (chunk + 1) * lines)
        restored_part[chunk_rows, (WAVES - 1) * wave :] = finish_sum(last_sums[chunk])
        new = lax.dot_general(
            restored_part[chunk_rows, :],
            basis_out_tile[...],
            (((1,), (1,)), ((), ())),
            preferred_element_type=F32,
        )

        def region(place, half, high):
            start = (high * 8 + place * 2 + c) * rows + chunk * lines
            if half is None:
                return gathered.at[pl.ds(pl.multiple_of(start, 16), lines), :]
            return gathered.at[pl.ds(pl.multiple_of(start + half * half_lines, 16), half_lines), :]

        own = Gather(pool, functools.partial(region, high=xh), z, z_up, z_down)
        other = Gather(pool, functools.partial(region, high=1 - xh), z, z_up, z_down)
        mine = region(z, None, xh)
        mine[...] = new.astype(BF16)
        across = Message(pool, mine, mine, x_far).start()
        own.start(0)
        own.start(1)
        pass_to_core(mine)
        ends.append((own, other, across, region))

    def start_other(chunk):
        own, other, across, region = ends[chunk]
        across.arrived()
        other.start(0)
        other.start(1)
        pass_to_core(region(z, None, 1 - xh))

    def forward(chunk, high):
        gather = ends[chunk][high]
        region = ends[chunk][3]
        gather.forward()
        gather.near()
        for place in (above, below):
            pass_to_core(region(place, None, xh if high == 0 else 1 - xh))

    def last(chunk, high):
        ends[chunk][high].far()
        pass_to_core(ends[chunk][3](far, None, xh if high == 0 else 1 - xh))

    for chunk in range(CHUNKS):
        finish_chunk(chunk)
        if chunk + 1 < CHUNKS:
            last_sums[chunk + 1].add()
        if chunk >= 1:
            forward(chunk - 1, 0)
            start_other(chunk - 1)
        if chunk >= 2:
            forward(chunk - 2, 1)
    forward(CHUNKS - 1, 0)
    start_other(CHUNKS - 1)
    if CHUNKS > 1:
        forward(CHUNKS - 2, 1)

    forward(CHUNKS - 1, 1)
    for chunk in range(CHUNKS):
        last(chunk, 0)
    cov_message.arrived()
    total = cov_scatter.total(xh) + cov_across[...].astype(F32)
    in_cov[:, :rows] = total[:rows]
    out_cov[:, :rows] = total[rows : rows + out_rows]
    out_cov[:, rows:] = total[rows + out_rows :]
    for half in range(2):
        right_scatter.arrived(half)
        in_cov[half * half_rows : (half + 1) * half_rows, rows:] = right_scatter.total(half)
    for chunk in range(CHUNKS):
        last(chunk, 1)

    for message in to_core_last:
        message.arrived()
    for own, other, across, region in ends:
        own.sent()
        other.sent()
        across.sent()
    for message in crossings + to_core_last + list(scatter_basis.values()) + small + turned_core:
        message.sent()
    for message in list(token_messages.values()) + [column_message, grad_message, cov_message, right_message]:
        message.sent()
    for group in [turned_gather, basis_gather, cov_scatter, right_scatter] + part_scatters + scaled_gathers + sums:
        group.sent()


def finish(gathered, in_cov, out_cov, old_in, old_out, precond, in_factor, out_factor, new_in, new_out, sem, tokens):
    copies = [pltpu.make_async_copy(gathered, precond, sem.at[0])]
    copies[0].start()
    new_in[...] = factor_decay * old_in[...] + (1.0 - factor_decay) * in_cov[...] / tokens
    new_out[...] = factor_decay * old_out[...] + (1.0 - factor_decay) * out_cov[...] / tokens
    copies += [pltpu.make_async_copy(new_in, in_factor, sem.at[1])]
    copies += [pltpu.make_async_copy(new_out, out_factor, sem.at[2])]
    for copy in copies[1:]:
        copy.start()
    for copy in copies:
        copy.wait()


def shards(
    inputs, out_grads, kernel_grad, basis_in, basis_out, eigen_in, eigen_out, old_in_factor, old_out_factor
):
    rows, width = kernel_grad.shape
    strip = basis_in.shape[0]
    tokens = inputs.shape[0]
    out_rows = old_out_factor.shape[0]
    deep = rows + 2 * out_rows
    total = 16 * rows
    narrow = width // 4
    anywhere = pl.BlockSpec(memory_space=pl.ANY)
    vmem = pl.BlockSpec(memory_space=pltpu.VMEM)
    scratch = [
        pltpu.VMEM((4, rows, 2 * rows), BF16),
        pltpu.VMEM((2, 4, rows, width), BF16),
        pltpu.VMEM((2, 4 * narrow, width), BF16),
        pltpu.VMEM((WAVES, 2, narrow, width // WAVES), BF16),
        pltpu.VMEM((WAVES, 4, narrow, width // WAVES), BF16),
        pltpu.VMEM((2, 4 * narrow, width), BF16),
        pltpu.VMEM((4, 8, rows), F32),
        pltpu.VMEM((2, 8, width), F32),
        pltpu.VMEM((WAVES, 4, rows, width // WAVES), BF16),
        pltpu.VMEM((WAVES, 4, rows, width // WAVES), BF16),
        pltpu.VMEM((4, rows, width // WAVES), F32),
        pltpu.VMEM((WAVES, 4, rows, width // WAVES), BF16),
        pltpu.VMEM((rows, width), BF16),
        pltpu.VMEM((WAVES, 2, rows // 2, width // WAVES), BF16),
        pltpu.VMEM((WAVES, 4, rows // 2, width // WAVES), BF16),
        pltpu.VMEM((2, 8, tokens, rows), BF16),
        pltpu.VMEM((2, tokens, width), BF16),
        pltpu.VMEM((2, tokens, width), BF16),
        pltpu.VMEM((width, width), BF16),
        pltpu.VMEM((2, 4, deep, rows), BF16),
        pltpu.VMEM((2, deep, rows), BF16),
        pltpu.VMEM((4, deep, rows), BF16),
        pltpu.VMEM((deep, rows), BF16),
        pltpu.VMEM((2, 4, rows, rows), BF16),
        pltpu.VMEM((4, rows, rows), BF16),
        pltpu.VMEM((2, rows // 2, rows), BF16),
        pltpu.VMEM((4, rows // 2, rows), BF16),
        pltpu.VMEM((rows, width), BF16),
        pltpu.VMEM((width, width), BF16),
        pltpu.SemaphoreType.DMA((16,)),
        pltpu.SemaphoreType.DMA((MESSAGES,)),
        pltpu.SemaphoreType.DMA((MESSAGES,)),
    ]
    gathered, in_cov, out_cov = pl.pallas_call(
        kernel,
        out_shape=(
            pltpu.VMEM((total, width), BF16),
            pltpu.VMEM((rows, width), F32),
            pltpu.VMEM((out_rows, width), F32),
        ),
        in_specs=[anywhere] * 5 + [vmem] * 2,
        out_specs=(vmem, vmem, vmem),
        scratch_shapes=scratch,
        compiler_params=pltpu.CompilerParams(
            collective_id=0, has_side_effects=True, vmem_limit_bytes=52 * 2**20
        ),
        cost_estimate=pl.CostEstimate(flops=2 * 10**10, bytes_accessed=4 * 10**7, transcendentals=0),
        name="precondition",
    )(
        inputs,
        out_grads,
        kernel_grad,
        basis_in,
        basis_out,
        eigen_in,
        eigen_out,
    )
    return pl.pallas_call(
        functools.partial(finish, tokens=16 * tokens),
        out_shape=(
            jax.ShapeDtypeStruct((total, width), BF16),
            jax.ShapeDtypeStruct((rows, width), F32),
            jax.ShapeDtypeStruct((out_rows, width), F32),
        ),
        in_specs=[vmem] * 5,
        out_specs=(anywhere, anywhere, anywhere),
        scratch_shapes=[pltpu.VMEM((rows, width), F32), pltpu.VMEM((out_rows, width), F32), pltpu.SemaphoreType.DMA((3,))],
        compiler_params=pltpu.CompilerParams(vmem_limit_bytes=40 * 2**20),
        name="finish",
    )(gathered, in_cov, out_cov, old_in_factor, old_out_factor)


def solution(mesh):
    in_specs = (
        P("dp", None),
        P("dp", None),
        P("dp", "owner"),
        P(("dp", "owner"), None),
        P("owner", None),
        P("dp"),
        P("owner"),
        P("dp", "owner"),
        P(("owner", "dp"), None),
    )
    out_specs = (P(None, "owner"), P("dp", "owner"), P(("owner", "dp"), None))
    return jax.shard_map(shards, mesh=mesh, in_specs=in_specs, out_specs=out_specs, check_vma=False)
```

```python
import functools

import jax
import jax.numpy as jnp
from jax import lax
from jax.experimental import pallas as pl
from jax.experimental.pallas import tpu as pltpu
from jax.sharding import PartitionSpec as P

damping = 0.3
factor_decay = 0.9
MESH = pl.DeviceIdType.MESH
CHUNKS = 3
CROSSED = 1
WAVES = 2
MESSAGES = 256
F32 = jnp.float32
BF16 = jnp.bfloat16


def dot_rows(left, right):
    return lax.dot_general(left, right, (((0,), (0,)), ((), ())), preferred_element_type=F32)


def dot(left, right):
    return jnp.dot(left, right, preferred_element_type=F32)


class Message:
    def __init__(self, pool, source, target, to):
        number = pool[2]
        pool[2] += 1
        self.copy = pltpu.make_async_remote_copy(
            src_ref=source,
            dst_ref=target,
            send_sem=pool[0].at[number],
            recv_sem=pool[1].at[number],
            device_id=to,
            device_id_type=MESH,
        )

    def start(self):
        self.copy.start()
        return self

    def arrived(self):
        self.copy.wait_recv()

    def sent(self):
        self.copy.wait_send()


class Gather:
    def __init__(self, pool, region, place, plus, minus):
        self.region, self.place, self.plus, self.minus, self.pool = region, place, plus, minus, pool
        self.own = {}
        self.passed = []

    def message(self, shard, half, to):
        piece = self.region(shard, half)
        return Message(self.pool, piece, piece, to).start()

    def start(self, half):
        order = (("plus", self.plus), ("minus", self.minus))
        for name, to in order if half == 0 else order[::-1]:
            self.own[name, half] = self.message(self.place, half, to)

    def forward(self):
        below, above = lax.rem(self.place + 3, 4), lax.rem(self.place + 1, 4)
        self.own["plus", 0].arrived()
        self.passed.append(self.message(below, 0, self.plus))
        self.own["minus", 1].arrived()
        self.passed.append(self.message(above, 1, self.minus))

    def near(self):
        self.own["minus", 0].arrived()
        self.own["plus", 1].arrived()

    def far(self):
        for message in self.passed:
            message.arrived()

    def sent(self):
        for message in list(self.own.values()) + self.passed:
            message.sent()


class Scatter:
    def __init__(self, pool, mine, transit, slots, place, plus, minus):
        self.pool, self.mine, self.transit, self.slots = pool, mine, transit, slots
        self.plus, self.minus = plus, minus
        self.here = place
        self.above, self.below, self.far = (lax.rem(place + step, 4) for step in (1, 3, 2))
        self.messages = []

    def send(self, source, target, to):
        message = Message(self.pool, source, target, to).start()
        self.messages.append(message)
        return message

    def start_far(self):
        self.up = self.send(self.mine(self.far, 0), self.transit(0), self.plus)
        self.down = self.send(self.mine(self.far, 1), self.transit(1), self.minus)

    def start_near(self):
        self.direct_up = self.send(self.mine(self.above, 1), self.slots(0), self.plus)
        self.direct_down = self.send(self.mine(self.below, 0), self.slots(1), self.minus)

    def add(self):
        for message, half, place in ((self.up, 0, self.above), (self.down, 1, self.below)):
            message.arrived()
            piece = self.mine(place, half)
            piece[...] = (piece[...].astype(F32) + self.transit(half)[...].astype(F32)).astype(BF16)
            if half == 0:
                self.pass_up()
        self.pass_down()

    def pass_up(self):
        self.sum_up = self.send(self.mine(self.above, 0), self.slots(2), self.plus)

    def pass_down(self):
        self.sum_down = self.send(self.mine(self.below, 1), self.slots(3), self.minus)

    def arrived(self, half):
        if half == 0:
            self.direct_down.arrived()
            self.sum_up.arrived()
        else:
            self.direct_up.arrived()
            self.sum_down.arrived()

    def total(self, half):
        return (
            self.mine(self.here, half)[...].astype(F32)
            + self.slots(1 - half)[...].astype(F32)
            + self.slots(2 + half)[...].astype(F32)
        )

    def sent(self):
        for message in self.messages:
            message.sent()


def kernel(
    inputs,
    grads,
    kernel_grad,
    basis_in,
    basis_out,
    eigen_in,
    eigen_out,
    gathered,
    in_cov,
    out_cov,
    basis,
    turned,
    part,
    part_transit,
    part_slots,
    scaled,
    eigen_rows,
    eigen_columns,
    away,
    away_in,
    home,
    home_sum,
    restored_part,
    home_transit,
    home_slots,
    tokens,
    token_columns,
    grad_columns,
    grad_part,
    cov,
    cov_transit,
    cov_slots,
    cov_across,
    right,
    right_in,
    right_transit,
    right_slots,
    grad_tile,
    basis_out_tile,
    local,
    send,
    receive,
):
    pool = [send, receive, 0]
    rows = kernel_grad.shape[0]
    width = kernel_grad.shape[1]
    strip = basis_in.shape[0]
    out_rows = out_cov.shape[0]
    narrow = width // 4
    dp, owner = lax.axis_index("dp"), lax.axis_index("owner")
    xh, z, c = dp // 8, lax.rem(dp // 2, 4), lax.rem(dp, 2)
    y, xl = owner // 2, lax.rem(owner, 2)
    x = xh * 2 + xl

    def device(x, y, z, c):
        x, y, z, c = lax.rem(x, 4), lax.rem(y, 4), lax.rem(z, 4), lax.rem(c, 2)
        return (x // 2) * 8 + z * 2 + c, y * 2 + lax.rem(x, 2)

    x_up, x_down, x_far = device(x + 1, y, z, c), device(x + 3, y, z, c), device(x + 2, y, z, c)
    y_up, y_down = device(x, y + 1, z, c), device(x, y + 3, z, c)
    z_up, z_down, z_far = device(x, y, z + 1, c), device(x, y, z + 3, c), device(x, y, z + 2, c)
    core = device(x, y, z, c + 1)
    pair = xh * 2 + 1 - xl
    cross = lax.rem(x + 2 * xl + 3, 4)
    plane = [(step, side) for step in (-1, 0, -2, 2) for side in (0, 1) if (step, side) != (0, 0)]
    x_pair = device(pair, y, z, c)

    locals_started = []

    def fetch(source, target):
        copy = pltpu.make_async_copy(source, target, local.at[len(locals_started)])
        copy.start()
        locals_started.append(copy)
        return copy

    def block_columns(ref, block):
        return ref.at[:, pl.ds(pl.multiple_of(block * rows, rows), rows)]

    def owner_columns(ref):
        return ref.at[:, pl.ds(pl.multiple_of(owner * width, width), width)]

    got_grad = fetch(kernel_grad, grad_tile)
    got_basis_out = fetch(basis_out, basis_out_tile)

    barrier = pltpu.get_barrier_semaphore()
    partners = [device(x + step, y, z, c + side) for step in range(4) for side in range(2) if step + side > 0]
    partners += [y_up, y_down, z_up, z_down, z_far]
    for partner in partners:
        pl.semaphore_signal(barrier, inc=1, device_id=partner, device_id_type=MESH)

    def strip_rows(x, y, c):
        block = (x // 2) * 2 + c
        start = pl.multiple_of((y * 2 + lax.rem(x, 2)) * strip, strip)
        return block, pl.ds(start, strip)

    my_block, my_rows = strip_rows(x, y, c)

    def basis_piece(t):
        return basis.at[my_block, my_rows, t * rows : (t + 1) * rows]

    own_basis = [
        fetch(block_columns(basis_in, xh * 8 + (2 * xl + t) * 2 + c), basis_piece(t)) for t in range(2)
    ]
    far, above, below = lax.rem(z + 2, 4), lax.rem(z + 1, 4), lax.rem(z + 3, 4)
    order = [far, above, below, z]
    got_tokens = {}
    got_columns = fetch(owner_columns(inputs), token_columns.at[0])
    got_grad_columns = fetch(owner_columns(grads), grad_columns.at[0])
    for step in range(4):
        for high in range(2):
            got_tokens[step, high] = fetch(
                block_columns(inputs, high * 8 + order[step] * 2 + c), tokens.at[0, step * 2 + high]
            )

    pl.semaphore_wait(barrier, len(partners))

    scatter_basis = {}
    for step, side in plane:
        to = {-1: pair, -2: cross, 0: x, 2: lax.rem(x + 2, 4)}[step]
        to_c = lax.rem(c + side, 2)
        for t in range(2):
            block = (to // 2) * 8 + (2 * lax.rem(to, 2) + t) * 2 + to_c
            scatter_basis[step, side, t] = Message(
                pool, block_columns(basis_in, block), basis_piece(t), device(to, y, z, to_c)
            ).start()
    small = []
    eigen_rows[z] = jnp.broadcast_to(eigen_in[...].reshape(1, rows), (8, rows))
    eigen_columns[xl] = jnp.broadcast_to(eigen_out[...].reshape(1, width), (8, width))
    for to in (z_up, z_down, z_far):
        small.append(Message(pool, eigen_rows.at[z], eigen_rows.at[z], to).start())
    small.append(Message(pool, eigen_columns.at[xl], eigen_columns.at[xl], x_pair).start())

    token_messages = {}
    column_message = Message(pool, owner_columns(inputs), token_columns.at[1], core).start()
    grad_message = Message(pool, owner_columns(grads), grad_columns.at[1], core).start()
    for step in range(4):
        for high in range(2):
            token_messages[step, high] = Message(
                pool,
                block_columns(inputs, high * 8 + order[step] * 2 + 1 - c),
                tokens.at[1, step * 2 + high],
                core,
            ).start()

    got_grad.wait()
    got_basis_out.wait()

    def turned_tile(x, c):
        return turned.at[lax.rem(x, 2), (x // 2) * 2 + c]

    turned_tile(x, c)[...] = dot(grad_tile[...], basis_out_tile[...]).astype(BF16)
    half_rows = rows // 2

    def turned_region(place, half):
        return turned.at[lax.rem(place, 2), (place // 2) * 2 + c, half * half_rows : (half + 1) * half_rows]

    def to_core(step):
        tile = turned_tile(lax.rem(x + step, 4), c)
        return Message(pool, tile, tile, core).start()

    turned_gather = Gather(pool, turned_region, x, x_up, x_down)

    def basis_region(place, half):
        start = pl.multiple_of(place * 2 * strip, 2 * strip)
        high = 2 * lax.rem(xh + half, 2)
        return basis.at[pl.ds(high, 2), pl.ds(start, 2 * strip), :]

    basis_gather = Gather(pool, basis_region, y, y_up, y_down)
    for copy in own_basis:
        copy.wait()
    for (step, side, t), message in scatter_basis.items():
        if step in (-1, 0):
            message.arrived()
    basis_gather.start(0)
    turned_gather.start(0)
    def cov_mine(place, half):
        return cov.at[half, place]

    cov_scatter = Scatter(
        pool, cov_mine, lambda half: cov_transit.at[half], lambda slot: cov_slots.at[slot], z, z_up, z_down
    )
    half_rows = rows // 2

    def right_mine(place, half):
        return right.at[xh, place, half * half_rows : (half + 1) * half_rows, :]

    right_scatter = Scatter(
        pool, right_mine, lambda half: right_transit.at[half], lambda slot: right_slots.at[slot], z, z_up, z_down
    )
    got_columns.wait()
    got_grad_columns.wait()
    column_message.arrived()
    grad_message.arrived()
    grad_part[...] = (
        dot_rows(grad_columns[0], grad_columns[0]) + dot_rows(grad_columns[1], grad_columns[1])
    ).astype(BF16)

    def cov_product(step):
        for high in range(2):
            got_tokens[step, high].wait()
            token_messages[step, high].arrived()
        place = order[step]

        def product(high, unused):
            tile = dot_rows(tokens[0, step * 2 + high], token_columns[0])
            tile = tile + dot_rows(tokens[1, step * 2 + high], token_columns[1])
            cov[high, place, :rows] = tile[:, :rows].astype(BF16)
            right[high, place] = tile[:, rows:].astype(BF16)
            start = pl.multiple_of((high * 8 + place * 2 + c) * out_rows, out_rows)
            cov[high, place, rows : rows + out_rows] = grad_part[pl.ds(start, out_rows), :rows]
            cov[high, place, rows + out_rows :] = grad_part[pl.ds(start, out_rows), rows:]
            return unused

        lax.fori_loop(0, 2, product, 0)

    cov_product(0)
    cov_scatter.start_far()
    for (step, side, t), message in scatter_basis.items():
        if step not in (-1, 0):
            message.arrived()
    basis_gather.start(1)
    turned_gather.start(1)
    turned_core = [to_core(0)]
    cov_product(1)
    cov_product(2)
    cov_scatter.start_near()
    turned_gather.forward()
    basis_gather.forward()
    cov_product(3)
    turned_gather.near()
    turned_core += [to_core(1), to_core(3)]
    right_message = Message(pool, right.at[1 - xh], right_in, x_far).start()
    cov_scatter.add()
    turned_gather.far()
    turned_core.append(to_core(2))
    basis_gather.near()
    basis_gather.far()
    for message in turned_core:
        message.arrived()

    wave = width // WAVES

    def rows_of(ref, place, half, number):
        start = pl.multiple_of(place * narrow, narrow)
        return ref.at[half, pl.ds(start, narrow), number * wave : (number + 1) * wave]

    part_scatters = [
        Scatter(
            pool,
            lambda place, half, number=number: rows_of(part, place, half, number),
            lambda half, number=number: part_transit.at[number, half],
            lambda slot, number=number: part_slots.at[number, slot],
            z,
            z_up,
            z_down,
        )
        for number in range(WAVES)
    ]

    def rotate(t, number):
        start = pl.multiple_of(t * rows, rows)
        left = basis[:, :, pl.ds(start, rows)].reshape(4 * rows, rows)

        def one(side, unused):
            right = turned[side, :, :, number * wave : (number + 1) * wave].reshape(4 * rows, wave)
            part[side, pl.ds(start, rows), number * wave : (number + 1) * wave] = dot_rows(left, right).astype(BF16)
            return unused

        lax.fori_loop(0, 2, one, 0)

    for number, scatter in enumerate(part_scatters):
        rotate(1 - z // 2, number)
        scatter.start_far()
        if number > 0:
            part_scatters[number - 1].add()
        rotate(z // 2, number)
        scatter.start_near()

    cov_scatter.arrived(0)
    cov_scatter.arrived(1)
    cov[1 - xh, z] = cov_scatter.total(1 - xh).astype(BF16)
    cov_message = Message(pool, cov.at[1 - xh, z], cov_across, x_far).start()

    for message in small:
        message.arrived()
    line = eigen_rows[2 * xl + z // 2]
    line = jnp.where(lax.rem(z, 2) == 0, line[:, :narrow], line[:, narrow:])
    column = jnp.transpose(jnp.broadcast_to(line[:1], (128, narrow)))[:, :1]

    scaled_gathers = []
    for number, scatter in enumerate(part_scatters):
        gather = Gather(
            pool, lambda place, half, number=number: rows_of(scaled, place, half, number), z, z_up, z_down
        )
        for half in range(2):
            scatter.arrived(half)
            divisor = column * eigen_columns[half, :1, number * wave : (number + 1) * wave] + damping
            rows_of(scaled, z, half, number)[...] = (scatter.total(half) / divisor).astype(BF16)
            gather.start(half)
        scaled_gathers.append(gather)
        if number + 1 < WAVES:
            if number + 2 == WAVES:
                part_scatters[number + 1].add()
            gather.forward()

    lines = rows // CHUNKS
    half_lines = lines // 2
    crossings, sums, ends, to_core_last = [], [], [], []

    def pass_to_core(ref):
        to_core_last.append(Message(pool, ref, ref, core).start())

    def start_sum(number, start, size):
        chunk_rows = slice(start, start + size)

        def partial(side, target):
            def one(place, unused):
                left = basis[(place // 2) * 2 + side, chunk_rows, :]
                right = scaled[lax.rem(place, 2), :, number * wave : (number + 1) * wave]
                target[place, chunk_rows, :] = dot(left, right).astype(target.dtype)
                return unused

            lax.fori_loop(0, 4, one, 0)

        partial(1 - c, away.at[number])
        crossing = Message(
            pool, away.at[number, :, chunk_rows, :], away_in.at[number, :, chunk_rows, :], core
        ).start()
        crossings.append(crossing)
        partial(c, home)

        def cross():
            crossing.arrived()
            home_sum[number, :, chunk_rows, :] = (
                home[:, chunk_rows, :] + away_in[number, :, chunk_rows, :].astype(F32)
            ).astype(BF16)
            half = size // 2
            scatter = Scatter(
                pool,
                lambda place, part_of: home_sum.at[
                    number, place, start + part_of * half : start + (part_of + 1) * half, :
                ],
                lambda part_of: home_transit.at[number, part_of, start // 2 : start // 2 + half, :],
                lambda slot: home_slots.at[number, slot, start // 2 : start // 2 + half, :],
                x,
                x_up,
                x_down,
            )
            scatter.start_far()
            scatter.start_near()
            sums.append(scatter)

        return cross

    def finish_sum(scatter):
        scatter.arrived(0)
        scatter.arrived(1)
        return jnp.concatenate([scatter.total(0), scatter.total(1)], axis=0).astype(BF16)

    right_message.arrived()
    right[xh] = (right[xh].astype(F32) + right_in[...].astype(F32)).astype(BF16)

    scaled_gathers[0].near()
    scaled_gathers[0].far()
    cross = start_sum(0, 0, rows)
    scaled_gathers[1].forward()
    cross()
    right_scatter.start_far()
    right_scatter.start_near()
    sums[0].add()
    scaled_gathers[1].near()
    scaled_gathers[1].far()
    crosses = [start_sum(1, 0, lines)]
    for chunk in range(CHUNKS):
        if chunk + 1 < CHUNKS:
            crosses.append(start_sum(1, (chunk + 1) * lines, lines))
        crosses[chunk]()
        if chunk == 1:
            right_scatter.add()
            sums[1].add()
    restored_part[:, :wave] = finish_sum(sums[0])
    last_sums = sums[1:]

    def finish_chunk(chunk):
        chunk_rows = slice(chunk * lines, (chunk + 1) * lines)
        restored_part[chunk_rows, (WAVES - 1) * wave :] = finish_sum(last_sums[chunk])
        new = lax.dot_general(
            restored_part[chunk_rows, :],
            basis_out_tile[...],
            (((1,), (1,)), ((), ())),
            preferred_element_type=F32,
        )

        def region(place, half, high):
            start = (high * 8 + place * 2 + c) * rows + chunk * lines
            if half is None:
                return gathered.at[pl.ds(pl.multiple_of(start, 16), lines), :]
            return gathered.at[pl.ds(pl.multiple_of(start + half * half_lines, 16), half_lines), :]

        own = Gather(pool, functools.partial(region, high=xh), z, z_up, z_down)
        other = Gather(pool, functools.partial(region, high=1 - xh), z, z_up, z_down)
        mine = region(z, None, xh)
        mine[...] = new.astype(BF16)
        across = Message(pool, mine, mine, x_far).start()
        own.start(0)
        own.start(1)
        pass_to_core(mine)
        ends.append((own, other, across, region))

    def start_other(chunk):
        own, other, across, region = ends[chunk]
        across.arrived()
        if chunk >= CROSSED:
            other.start(0)
            other.start(1)
        pass_to_core(region(z, None, 1 - xh))

    crossed = {}

    def cross_over(chunk, place, name):
        ref = ends[chunk][3](place, None, xh)
        crossed[chunk, name] = Message(pool, ref, ref, x_far).start()

    def crossed_over(chunk, place, name):
        crossed[chunk, name].arrived()
        pass_to_core(ends[chunk][3](place, None, 1 - xh))

    def forward(chunk, high):
        gather = ends[chunk][high]
        region = ends[chunk][3]
        if high == 1 and chunk < CROSSED:
            return
        gather.forward()
        gather.near()
        for place in (above, below):
            pass_to_core(region(place, None, xh if high == 0 else 1 - xh))

    def last(chunk, high):
        if high == 1 and chunk < CROSSED:
            crossed_over(chunk, above, "above")
            crossed_over(chunk, below, "below")
            crossed_over(chunk, far, "far")
            return
        ends[chunk][high].far()
        if chunk < CROSSED:
            cross_over(chunk, far, "far")
        pass_to_core(ends[chunk][3](far, None, xh if high == 0 else 1 - xh))

    for chunk in range(CHUNKS):
        finish_chunk(chunk)
        if chunk + 1 < CHUNKS:
            last_sums[chunk + 1].add()
        if chunk >= 1:
            forward(chunk - 1, 0)
            start_other(chunk - 1)
        if chunk >= 2:
            forward(chunk - 2, 1)
    for chunk in range(CROSSED):
        cross_over(chunk, above, "above")
        cross_over(chunk, below, "below")
    forward(CHUNKS - 1, 0)
    start_other(CHUNKS - 1)
    for chunk in range(CROSSED):
        last(chunk, 0)
    if CHUNKS > 1:
        forward(CHUNKS - 2, 1)

    forward(CHUNKS - 1, 1)
    for chunk in range(CROSSED, CHUNKS):
        last(chunk, 0)
    cov_message.arrived()
    total = cov_scatter.total(xh) + cov_across[...].astype(F32)
    in_cov[:, :rows] = total[:rows]
    out_cov[:, :rows] = total[rows : rows + out_rows]
    out_cov[:, rows:] = total[rows + out_rows :]
    for half in range(2):
        right_scatter.arrived(half)
        in_cov[half * half_rows : (half + 1) * half_rows, rows:] = right_scatter.total(half)
    for chunk in range(CHUNKS):
        last(chunk, 1)

    for message in to_core_last:
        message.arrived()
    for own, other, across, region in ends:
        own.sent()
        other.sent()
        across.sent()
    for message in list(crossed.values()) + crossings + to_core_last + list(scatter_basis.values()) + small + turned_core:
        message.sent()
    for message in list(token_messages.values()) + [column_message, grad_message, cov_message, right_message]:
        message.sent()
    for group in [turned_gather, basis_gather, cov_scatter, right_scatter] + part_scatters + scaled_gathers + sums:
        group.sent()


def finish(gathered, in_cov, out_cov, old_in, old_out, precond, in_factor, out_factor, new_in, new_out, sem, tokens):
    copies = [pltpu.make_async_copy(gathered, precond, sem.at[0])]
    copies[0].start()
    new_in[...] = factor_decay * old_in[...] + (1.0 - factor_decay) * in_cov[...] / tokens
    new_out[...] = factor_decay * old_out[...] + (1.0 - factor_decay) * out_cov[...] / tokens
    copies += [pltpu.make_async_copy(new_in, in_factor, sem.at[1])]
    copies += [pltpu.make_async_copy(new_out, out_factor, sem.at[2])]
    for copy in copies[1:]:
        copy.start()
    for copy in copies:
        copy.wait()


def shards(
    inputs, out_grads, kernel_grad, basis_in, basis_out, eigen_in, eigen_out, old_in_factor, old_out_factor
):
    rows, width = kernel_grad.shape
    strip = basis_in.shape[0]
    tokens = inputs.shape[0]
    out_rows = old_out_factor.shape[0]
    deep = rows + 2 * out_rows
    total = 16 * rows
    narrow = width // 4
    anywhere = pl.BlockSpec(memory_space=pl.ANY)
    vmem = pl.BlockSpec(memory_space=pltpu.VMEM)
    scratch = [
        pltpu.VMEM((4, rows, 2 * rows), BF16),
        pltpu.VMEM((2, 4, rows, width), BF16),
        pltpu.VMEM((2, 4 * narrow, width), BF16),
        pltpu.VMEM((WAVES, 2, narrow, width // WAVES), BF16),
        pltpu.VMEM((WAVES, 4, narrow, width // WAVES), BF16),
        pltpu.VMEM((2, 4 * narrow, width), BF16),
        pltpu.VMEM((4, 8, rows), F32),
        pltpu.VMEM((2, 8, width), F32),
        pltpu.VMEM((WAVES, 4, rows, width // WAVES), BF16),
        pltpu.VMEM((WAVES, 4, rows, width // WAVES), BF16),
        pltpu.VMEM((4, rows, width // WAVES), F32),
        pltpu.VMEM((WAVES, 4, rows, width // WAVES), BF16),
        pltpu.VMEM((rows, width), BF16),
        pltpu.VMEM((WAVES, 2, rows // 2, width // WAVES), BF16),
        pltpu.VMEM((WAVES, 4, rows // 2, width // WAVES), BF16),
        pltpu.VMEM((2, 8, tokens, rows), BF16),
        pltpu.VMEM((2, tokens, width), BF16),
        pltpu.VMEM((2, tokens, width), BF16),
        pltpu.VMEM((width, width), BF16),
        pltpu.VMEM((2, 4, deep, rows), BF16),
        pltpu.VMEM((2, deep, rows), BF16),
        pltpu.VMEM((4, deep, rows), BF16),
        pltpu.VMEM((deep, rows), BF16),
        pltpu.VMEM((2, 4, rows, rows), BF16),
        pltpu.VMEM((4, rows, rows), BF16),
        pltpu.VMEM((2, rows // 2, rows), BF16),
        pltpu.VMEM((4, rows // 2, rows), BF16),
        pltpu.VMEM((rows, width), BF16),
        pltpu.VMEM((width, width), BF16),
        pltpu.SemaphoreType.DMA((16,)),
        pltpu.SemaphoreType.DMA((MESSAGES,)),
        pltpu.SemaphoreType.DMA((MESSAGES,)),
    ]
    gathered, in_cov, out_cov = pl.pallas_call(
        kernel,
        out_shape=(
            pltpu.VMEM((total, width), BF16),
            pltpu.VMEM((rows, width), F32),
            pltpu.VMEM((out_rows, width), F32),
        ),
        in_specs=[anywhere] * 5 + [vmem] * 2,
        out_specs=(vmem, vmem, vmem),
        scratch_shapes=scratch,
        compiler_params=pltpu.CompilerParams(
            collective_id=0, has_side_effects=True, vmem_limit_bytes=52 * 2**20
        ),
        cost_estimate=pl.CostEstimate(flops=2 * 10**10, bytes_accessed=4 * 10**7, transcendentals=0),
        name="precondition",
    )(
        inputs,
        out_grads,
        kernel_grad,
        basis_in,
        basis_out,
        eigen_in,
        eigen_out,
    )
    return pl.pallas_call(
        functools.partial(finish, tokens=16 * tokens),
        out_shape=(
            jax.ShapeDtypeStruct((total, width), BF16),
            jax.ShapeDtypeStruct((rows, width), F32),
            jax.ShapeDtypeStruct((out_rows, width), F32),
        ),
        in_specs=[vmem] * 5,
        out_specs=(anywhere, anywhere, anywhere),
        scratch_shapes=[pltpu.VMEM((rows, width), F32), pltpu.VMEM((out_rows, width), F32), pltpu.SemaphoreType.DMA((3,))],
        compiler_params=pltpu.CompilerParams(vmem_limit_bytes=40 * 2**20),
        name="finish",
    )(gathered, in_cov, out_cov, old_in_factor, old_out_factor)


def solution(mesh):
    in_specs = (
        P("dp", None),
        P("dp", None),
        P("dp", "owner"),
        P(("dp", "owner"), None),
        P("owner", None),
        P("dp"),
        P("owner"),
        P("dp", "owner"),
        P(("owner", "dp"), None),
    )
    out_specs = (P(None, "owner"), P("dp", "owner"), P(("owner", "dp"), None))
    return jax.shard_map(shards, mesh=mesh, in_specs=in_specs, out_specs=out_specs, check_vma=False)
```

```python
import functools

import jax
import jax.numpy as jnp
from jax import lax
from jax.experimental import pallas as pl
from jax.experimental.pallas import tpu as pltpu
from jax.sharding import PartitionSpec as P

damping = 0.3
factor_decay = 0.9
MESH = pl.DeviceIdType.MESH
CHUNKS = 3
CROSSED = 1
WAVES = 2
MESSAGES = 256
F32 = jnp.float32
BF16 = jnp.bfloat16


def dot_rows(left, right):
    return lax.dot_general(left, right, (((0,), (0,)), ((), ())), preferred_element_type=F32)


def dot(left, right):
    return jnp.dot(left, right, preferred_element_type=F32)


class Message:
    def __init__(self, pool, source, target, to):
        number = pool[2]
        pool[2] += 1
        self.copy = pltpu.make_async_remote_copy(
            src_ref=source,
            dst_ref=target,
            send_sem=pool[0].at[number],
            recv_sem=pool[1].at[number],
            device_id=to,
            device_id_type=MESH,
        )

    def start(self):
        self.copy.start()
        return self

    def arrived(self):
        self.copy.wait_recv()

    def sent(self):
        self.copy.wait_send()


class Gather:
    def __init__(self, pool, region, place, plus, minus):
        self.region, self.place, self.plus, self.minus, self.pool = region, place, plus, minus, pool
        self.own = {}
        self.passed = []

    def message(self, shard, half, to):
        piece = self.region(shard, half)
        return Message(self.pool, piece, piece, to).start()

    def start(self, half):
        order = (("plus", self.plus), ("minus", self.minus))
        for name, to in order if half == 0 else order[::-1]:
            self.own[name, half] = self.message(self.place, half, to)

    def forward(self):
        below, above = lax.rem(self.place + 3, 4), lax.rem(self.place + 1, 4)
        self.own["plus", 0].arrived()
        self.passed.append(self.message(below, 0, self.plus))
        self.own["minus", 1].arrived()
        self.passed.append(self.message(above, 1, self.minus))

    def near(self):
        self.own["minus", 0].arrived()
        self.own["plus", 1].arrived()

    def far(self):
        for message in self.passed:
            message.arrived()

    def sent(self):
        for message in list(self.own.values()) + self.passed:
            message.sent()


class Scatter:
    def __init__(self, pool, mine, transit, slots, place, plus, minus):
        self.pool, self.mine, self.transit, self.slots = pool, mine, transit, slots
        self.plus, self.minus = plus, minus
        self.here = place
        self.above, self.below, self.far = (lax.rem(place + step, 4) for step in (1, 3, 2))
        self.messages = []

    def send(self, source, target, to):
        message = Message(self.pool, source, target, to).start()
        self.messages.append(message)
        return message

    def start_far(self):
        self.up = self.send(self.mine(self.far, 0), self.transit(0), self.plus)
        self.down = self.send(self.mine(self.far, 1), self.transit(1), self.minus)

    def start_near(self):
        self.direct_up = self.send(self.mine(self.above, 1), self.slots(0), self.plus)
        self.direct_down = self.send(self.mine(self.below, 0), self.slots(1), self.minus)

    def add(self):
        for message, half, place in ((self.up, 0, self.above), (self.down, 1, self.below)):
            message.arrived()
            piece = self.mine(place, half)
            piece[...] = (piece[...].astype(F32) + self.transit(half)[...].astype(F32)).astype(BF16)
            if half == 0:
                self.pass_up()
        self.pass_down()

    def pass_up(self):
        self.sum_up = self.send(self.mine(self.above, 0), self.slots(2), self.plus)

    def pass_down(self):
        self.sum_down = self.send(self.mine(self.below, 1), self.slots(3), self.minus)

    def arrived(self, half):
        if half == 0:
            self.direct_down.arrived()
            self.sum_up.arrived()
        else:
            self.direct_up.arrived()
            self.sum_down.arrived()

    def total(self, half):
        return (
            self.mine(self.here, half)[...].astype(F32)
            + self.slots(1 - half)[...].astype(F32)
            + self.slots(2 + half)[...].astype(F32)
        )

    def sent(self):
        for message in self.messages:
            message.sent()


def kernel(
    inputs,
    grads,
    kernel_grad,
    basis_in,
    basis_out,
    eigen_in,
    eigen_out,
    gathered,
    in_cov,
    out_cov,
    basis,
    turned,
    part,
    part_transit,
    part_slots,
    scaled,
    eigen_rows,
    eigen_columns,
    away,
    away_in,
    home,
    home_sum,
    restored_part,
    home_transit,
    home_slots,
    tokens,
    token_columns,
    grad_columns,
    grad_part,
    cov,
    cov_transit,
    cov_slots,
    cov_across,
    right,
    right_in,
    right_transit,
    right_slots,
    grad_tile,
    basis_out_tile,
    local,
    send,
    receive,
):
    pool = [send, receive, 0]
    rows = kernel_grad.shape[0]
    width = kernel_grad.shape[1]
    strip = basis_in.shape[0]
    out_rows = out_cov.shape[0]
    narrow = width // 4
    dp, owner = lax.axis_index("dp"), lax.axis_index("owner")
    xh, z, c = dp // 8, lax.rem(dp // 2, 4), lax.rem(dp, 2)
    y, xl = owner // 2, lax.rem(owner, 2)
    x = xh * 2 + xl

    def device(x, y, z, c):
        x, y, z, c = lax.rem(x, 4), lax.rem(y, 4), lax.rem(z, 4), lax.rem(c, 2)
        return (x // 2) * 8 + z * 2 + c, y * 2 + lax.rem(x, 2)

    x_up, x_down, x_far = device(x + 1, y, z, c), device(x + 3, y, z, c), device(x + 2, y, z, c)
    y_up, y_down = device(x, y + 1, z, c), device(x, y + 3, z, c)
    z_up, z_down, z_far = device(x, y, z + 1, c), device(x, y, z + 3, c), device(x, y, z + 2, c)
    core = device(x, y, z, c + 1)
    pair = xh * 2 + 1 - xl
    cross = lax.rem(x + 2 * xl + 3, 4)
    plane = [(step, side) for step in (-1, 0, -2, 2) for side in (0, 1) if (step, side) != (0, 0)]
    x_pair = device(pair, y, z, c)

    locals_started = []

    def fetch(source, target):
        copy = pltpu.make_async_copy(source, target, local.at[len(locals_started)])
        copy.start()
        locals_started.append(copy)
        return copy

    def block_columns(ref, block):
        return ref.at[:, pl.ds(pl.multiple_of(block * rows, rows), rows)]

    def owner_columns(ref):
        return ref.at[:, pl.ds(pl.multiple_of(owner * width, width), width)]

    got_grad = fetch(kernel_grad, grad_tile)
    got_basis_out = fetch(basis_out, basis_out_tile)

    barrier = pltpu.get_barrier_semaphore()
    partners = [device(x + step, y, z, c + side) for step in range(4) for side in range(2) if step + side > 0]
    partners += [y_up, y_down, z_up, z_down, z_far]
    for partner in partners:
        pl.semaphore_signal(barrier, inc=1, device_id=partner, device_id_type=MESH)

    def strip_rows(x, y, c):
        block = (x // 2) * 2 + c
        start = pl.multiple_of((y * 2 + lax.rem(x, 2)) * strip, strip)
        return block, pl.ds(start, strip)

    my_block, my_rows = strip_rows(x, y, c)

    def basis_piece(t):
        return basis.at[my_block, my_rows, t * rows : (t + 1) * rows]

    own_basis = [
        fetch(block_columns(basis_in, xh * 8 + (2 * xl + t) * 2 + c), basis_piece(t)) for t in range(2)
    ]
    far, above, below = lax.rem(z + 2, 4), lax.rem(z + 1, 4), lax.rem(z + 3, 4)
    order = [far, above, below, z]
    got_tokens = {}
    got_columns = fetch(owner_columns(inputs), token_columns.at[0])
    got_grad_columns = fetch(owner_columns(grads), grad_columns.at[0])
    for step in range(4):
        for high in range(2):
            got_tokens[step, high] = fetch(
                block_columns(inputs, high * 8 + order[step] * 2 + c), tokens.at[0, step * 2 + high]
            )

    pl.semaphore_wait(barrier, len(partners))

    scatter_basis = {}
    for step, side in plane:
        to = {-1: pair, -2: cross, 0: x, 2: lax.rem(x + 2, 4)}[step]
        to_c = lax.rem(c + side, 2)
        for t in range(2):
            block = (to // 2) * 8 + (2 * lax.rem(to, 2) + t) * 2 + to_c
            scatter_basis[step, side, t] = Message(
                pool, block_columns(basis_in, block), basis_piece(t), device(to, y, z, to_c)
            ).start()
    small = []
    eigen_rows[z] = jnp.broadcast_to(eigen_in[...].reshape(1, rows), (8, rows))
    eigen_columns[xl] = jnp.broadcast_to(eigen_out[...].reshape(1, width), (8, width))
    for to in (z_up, z_down, z_far):
        small.append(Message(pool, eigen_rows.at[z], eigen_rows.at[z], to).start())
    small.append(Message(pool, eigen_columns.at[xl], eigen_columns.at[xl], x_pair).start())

    token_messages = {}
    column_message = Message(pool, owner_columns(inputs), token_columns.at[1], core).start()
    grad_message = Message(pool, owner_columns(grads), grad_columns.at[1], core).start()
    for step in range(4):
        for high in range(2):
            token_messages[step, high] = Message(
                pool,
                block_columns(inputs, high * 8 + order[step] * 2 + 1 - c),
                tokens.at[1, step * 2 + high],
                core,
            ).start()

    got_grad.wait()
    got_basis_out.wait()

    def turned_tile(x, c):
        return turned.at[lax.rem(x, 2), (x // 2) * 2 + c]

    turned_tile(x, c)[...] = dot(grad_tile[...], basis_out_tile[...]).astype(BF16)
    half_rows = rows // 2

    def turned_region(place, half):
        return turned.at[lax.rem(place, 2), (place // 2) * 2 + c, half * half_rows : (half + 1) * half_rows]

    def to_core(step):
        tile = turned_tile(lax.rem(x + step, 4), c)
        return Message(pool, tile, tile, core).start()

    turned_gather = Gather(pool, turned_region, x, x_up, x_down)

    def basis_region(place, half):
        start = pl.multiple_of(place * 2 * strip, 2 * strip)
        high = 2 * lax.rem(xh + half, 2)
        return basis.at[pl.ds(high, 2), pl.ds(start, 2 * strip), :]

    basis_gather = Gather(pool, basis_region, y, y_up, y_down)
    for copy in own_basis:
        copy.wait()
    for (step, side, t), message in scatter_basis.items():
        if step in (-1, 0):
            message.arrived()
    basis_gather.start(0)
    turned_gather.start(0)
    def cov_mine(place, half):
        return cov.at[half, place]

    cov_scatter = Scatter(
        pool, cov_mine, lambda half: cov_transit.at[half], lambda slot: cov_slots.at[slot], z, z_up, z_down
    )
    half_rows = rows // 2

    def right_mine(place, half):
        return right.at[xh, place, half * half_rows : (half + 1) * half_rows, :]

    right_scatter = Scatter(
        pool, right_mine, lambda half: right_transit.at[half], lambda slot: right_slots.at[slot], z, z_up, z_down
    )
    got_columns.wait()
    got_grad_columns.wait()
    column_message.arrived()
    grad_message.arrived()
    grad_part[...] = (
        dot_rows(grad_columns[0], grad_columns[0]) + dot_rows(grad_columns[1], grad_columns[1])
    ).astype(BF16)

    def cov_product(step):
        for high in range(2):
            got_tokens[step, high].wait()
            token_messages[step, high].arrived()
        place = order[step]

        def product(high, unused):
            tile = dot_rows(tokens[0, step * 2 + high], token_columns[0])
            tile = tile + dot_rows(tokens[1, step * 2 + high], token_columns[1])
            cov[high, place, :rows] = tile[:, :rows].astype(BF16)
            right[high, place] = tile[:, rows:].astype(BF16)
            start = pl.multiple_of((high * 8 + place * 2 + c) * out_rows, out_rows)
            cov[high, place, rows : rows + out_rows] = grad_part[pl.ds(start, out_rows), :rows]
            cov[high, place, rows + out_rows :] = grad_part[pl.ds(start, out_rows), rows:]
            return unused

        lax.fori_loop(0, 2, product, 0)

    cov_product(0)
    cov_scatter.start_far()
    for (step, side, t), message in scatter_basis.items():
        if step not in (-1, 0):
            message.arrived()
    basis_gather.start(1)
    turned_gather.start(1)
    turned_core = [to_core(0)]
    cov_product(1)
    cov_product(2)
    cov_scatter.start_near()
    turned_gather.forward()
    basis_gather.forward()
    cov_product(3)
    turned_gather.near()
    turned_core += [to_core(1), to_core(3)]
    right_message = Message(pool, right.at[1 - xh], right_in, x_far).start()
    cov_scatter.add()
    turned_gather.far()
    turned_core.append(to_core(2))
    basis_gather.near()
    basis_gather.far()
    for message in turned_core:
        message.arrived()

    wave = width // WAVES

    def rows_of(ref, place, half, number):
        start = pl.multiple_of(place * narrow, narrow)
        return ref.at[half, pl.ds(start, narrow), number * wave : (number + 1) * wave]

    part_scatters = [
        Scatter(
            pool,
            lambda place, half, number=number: rows_of(part, place, half, number),
            lambda half, number=number: part_transit.at[number, half],
            lambda slot, number=number: part_slots.at[number, slot],
            z,
            z_up,
            z_down,
        )
        for number in range(WAVES)
    ]

    def rotate(t, number):
        start = pl.multiple_of(t * rows, rows)
        left = basis[:, :, pl.ds(start, rows)].reshape(4 * rows, rows)

        def one(side, unused):
            right = turned[side, :, :, number * wave : (number + 1) * wave].reshape(4 * rows, wave)
            part[side, pl.ds(start, rows), number * wave : (number + 1) * wave] = dot_rows(left, right).astype(BF16)
            return unused

        lax.fori_loop(0, 2, one, 0)

    for number, scatter in enumerate(part_scatters):
        rotate(1 - z // 2, number)
        scatter.start_far()
        if number > 0:
            part_scatters[number - 1].add()
        rotate(z // 2, number)
        scatter.start_near()

    cov_scatter.arrived(0)
    cov_scatter.arrived(1)
    cov[1 - xh, z] = cov_scatter.total(1 - xh).astype(BF16)
    cov_message = Message(pool, cov.at[1 - xh, z], cov_across, x_far).start()

    for message in small:
        message.arrived()
    line = eigen_rows[2 * xl + z // 2]
    line = jnp.where(lax.rem(z, 2) == 0, line[:, :narrow], line[:, narrow:])
    column = jnp.transpose(jnp.broadcast_to(line[:1], (128, narrow)))[:, :1]

    scaled_gathers = []
    for number, scatter in enumerate(part_scatters):
        gather = Gather(
            pool, lambda place, half, number=number: rows_of(scaled, place, half, number), z, z_up, z_down
        )
        for half in range(2):
            scatter.arrived(half)
            divisor = column * eigen_columns[half, :1, number * wave : (number + 1) * wave] + damping
            rows_of(scaled, z, half, number)[...] = (scatter.total(half) / divisor).astype(BF16)
            gather.start(half)
        scaled_gathers.append(gather)
        if number + 1 < WAVES:
            if number + 2 == WAVES:
                part_scatters[number + 1].add()
            gather.forward()

    lines = rows // CHUNKS
    half_lines = lines // 2
    crossings, sums, ends, to_core_last = [], [], [], []

    def pass_to_core(ref):
        to_core_last.append(Message(pool, ref, ref, core).start())

    def start_sum(number, start, size):
        chunk_rows = slice(start, start + size)

        def partial(side, target):
            def one(place, unused):
                left = basis[(place // 2) * 2 + side, chunk_rows, :]
                right = scaled[lax.rem(place, 2), :, number * wave : (number + 1) * wave]
                target[place, chunk_rows, :] = dot(left, right).astype(target.dtype)
                return unused

            lax.fori_loop(0, 4, one, 0)

        partial(1 - c, away.at[number])
        crossing = Message(
            pool, away.at[number, :, chunk_rows, :], away_in.at[number, :, chunk_rows, :], core
        ).start()
        crossings.append(crossing)
        partial(c, home)

        def cross():
            crossing.arrived()
            home_sum[number, :, chunk_rows, :] = (
                home[:, chunk_rows, :] + away_in[number, :, chunk_rows, :].astype(F32)
            ).astype(BF16)
            half = size // 2
            scatter = Scatter(
                pool,
                lambda place, part_of: home_sum.at[
                    number, place, start + part_of * half : start + (part_of + 1) * half, :
                ],
                lambda part_of: home_transit.at[number, part_of, start // 2 : start // 2 + half, :],
                lambda slot: home_slots.at[number, slot, start // 2 : start // 2 + half, :],
                x,
                x_up,
                x_down,
            )
            scatter.start_far()
            scatter.start_near()
            sums.append(scatter)

        return cross

    def finish_sum(scatter):
        scatter.arrived(0)
        scatter.arrived(1)
        return jnp.concatenate([scatter.total(0), scatter.total(1)], axis=0).astype(BF16)

    right_message.arrived()
    right[xh] = (right[xh].astype(F32) + right_in[...].astype(F32)).astype(BF16)

    scaled_gathers[0].near()
    scaled_gathers[0].far()
    cross = start_sum(0, 0, rows)
    scaled_gathers[1].forward()
    cross()
    right_scatter.start_far()
    right_scatter.start_near()
    sums[0].add()
    scaled_gathers[1].near()
    scaled_gathers[1].far()
    crosses = [start_sum(1, 0, lines)]
    for chunk in range(CHUNKS):
        if chunk + 1 < CHUNKS:
            crosses.append(start_sum(1, (chunk + 1) * lines, lines))
        if chunk == 1:
            sums[1].add()
        crosses[chunk]()
        if chunk == CHUNKS - 1:
            right_scatter.add()
    restored_part[:, :wave] = finish_sum(sums[0])
    last_sums = sums[1:]

    def finish_chunk(chunk):
        chunk_rows = slice(chunk * lines, (chunk + 1) * lines)
        restored_part[chunk_rows, (WAVES - 1) * wave :] = finish_sum(last_sums[chunk])
        new = lax.dot_general(
            restored_part[chunk_rows, :],
            basis_out_tile[...],
            (((1,), (1,)), ((), ())),
            preferred_element_type=F32,
        )

        def region(place, half, high):
            start = (high * 8 + place * 2 + c) * rows + chunk * lines
            if half is None:
                return gathered.at[pl.ds(pl.multiple_of(start, 16), lines), :]
            return gathered.at[pl.ds(pl.multiple_of(start + half * half_lines, 16), half_lines), :]

        own = Gather(pool, functools.partial(region, high=xh), z, z_up, z_down)
        other = Gather(pool, functools.partial(region, high=1 - xh), z, z_up, z_down)
        mine = region(z, None, xh)
        mine[...] = new.astype(BF16)
        across = Message(pool, mine, mine, x_far).start()
        own.start(0)
        own.start(1)
        pass_to_core(mine)
        ends.append((own, other, across, region))

    def start_other(chunk):
        own, other, across, region = ends[chunk]
        across.arrived()
        if chunk >= CROSSED:
            other.start(0)
            other.start(1)
        pass_to_core(region(z, None, 1 - xh))

    crossed = {}

    def cross_over(chunk, place, name):
        ref = ends[chunk][3](place, None, xh)
        crossed[chunk, name] = Message(pool, ref, ref, x_far).start()

    def crossed_over(chunk, place, name):
        crossed[chunk, name].arrived()
        pass_to_core(ends[chunk][3](place, None, 1 - xh))

    def forward(chunk, high):
        gather = ends[chunk][high]
        region = ends[chunk][3]
        if high == 1 and chunk < CROSSED:
            return
        gather.forward()
        gather.near()
        for place in (above, below):
            pass_to_core(region(place, None, xh if high == 0 else 1 - xh))

    def last(chunk, high):
        if high == 1 and chunk < CROSSED:
            crossed_over(chunk, above, "above")
            crossed_over(chunk, below, "below")
            crossed_over(chunk, far, "far")
            return
        ends[chunk][high].far()
        if chunk < CROSSED:
            cross_over(chunk, far, "far")
        pass_to_core(ends[chunk][3](far, None, xh if high == 0 else 1 - xh))

    for chunk in range(CHUNKS):
        finish_chunk(chunk)
        if chunk + 1 < CHUNKS:
            last_sums[chunk + 1].add()
        if chunk >= 1:
            forward(chunk - 1, 0)
            start_other(chunk - 1)
        if chunk >= 2:
            forward(chunk - 2, 1)
    for chunk in range(CROSSED):
        cross_over(chunk, above, "above")
        cross_over(chunk, below, "below")
    forward(CHUNKS - 1, 0)
    start_other(CHUNKS - 1)
    for chunk in range(CROSSED):
        last(chunk, 0)
    if CHUNKS > 1:
        forward(CHUNKS - 2, 1)

    forward(CHUNKS - 1, 1)
    for chunk in range(CROSSED, CHUNKS):
        last(chunk, 0)
    cov_message.arrived()
    total = cov_scatter.total(xh) + cov_across[...].astype(F32)
    in_cov[:, :rows] = total[:rows]
    out_cov[:, :rows] = total[rows : rows + out_rows]
    out_cov[:, rows:] = total[rows + out_rows :]
    for half in range(2):
        right_scatter.arrived(half)
        in_cov[half * half_rows : (half + 1) * half_rows, rows:] = right_scatter.total(half)
    for chunk in range(CHUNKS):
        last(chunk, 1)

    for message in to_core_last:
        message.arrived()
    for own, other, across, region in ends:
        own.sent()
        other.sent()
        across.sent()
    for message in list(crossed.values()) + crossings + to_core_last + list(scatter_basis.values()) + small + turned_core:
        message.sent()
    for message in list(token_messages.values()) + [column_message, grad_message, cov_message, right_message]:
        message.sent()
    for group in [turned_gather, basis_gather, cov_scatter, right_scatter] + part_scatters + scaled_gathers + sums:
        group.sent()


def finish(gathered, in_cov, out_cov, old_in, old_out, precond, in_factor, out_factor, new_in, new_out, sem, tokens):
    copies = [pltpu.make_async_copy(gathered, precond, sem.at[0])]
    copies[0].start()
    new_in[...] = factor_decay * old_in[...] + (1.0 - factor_decay) * in_cov[...] / tokens
    new_out[...] = factor_decay * old_out[...] + (1.0 - factor_decay) * out_cov[...] / tokens
    copies += [pltpu.make_async_copy(new_in, in_factor, sem.at[1])]
    copies += [pltpu.make_async_copy(new_out, out_factor, sem.at[2])]
    for copy in copies[1:]:
        copy.start()
    for copy in copies:
        copy.wait()


def shards(
    inputs, out_grads, kernel_grad, basis_in, basis_out, eigen_in, eigen_out, old_in_factor, old_out_factor
):
    rows, width = kernel_grad.shape
    strip = basis_in.shape[0]
    tokens = inputs.shape[0]
    out_rows = old_out_factor.shape[0]
    deep = rows + 2 * out_rows
    total = 16 * rows
    narrow = width // 4
    anywhere = pl.BlockSpec(memory_space=pl.ANY)
    vmem = pl.BlockSpec(memory_space=pltpu.VMEM)
    scratch = [
        pltpu.VMEM((4, rows, 2 * rows), BF16),
        pltpu.VMEM((2, 4, rows, width), BF16),
        pltpu.VMEM((2, 4 * narrow, width), BF16),
        pltpu.VMEM((WAVES, 2, narrow, width // WAVES), BF16),
        pltpu.VMEM((WAVES, 4, narrow, width // WAVES), BF16),
        pltpu.VMEM((2, 4 * narrow, width), BF16),
        pltpu.VMEM((4, 8, rows), F32),
        pltpu.VMEM((2, 8, width), F32),
        pltpu.VMEM((WAVES, 4, rows, width // WAVES), BF16),
        pltpu.VMEM((WAVES, 4, rows, width // WAVES), BF16),
        pltpu.VMEM((4, rows, width // WAVES), F32),
        pltpu.VMEM((WAVES, 4, rows, width // WAVES), BF16),
        pltpu.VMEM((rows, width), BF16),
        pltpu.VMEM((WAVES, 2, rows // 2, width // WAVES), BF16),
        pltpu.VMEM((WAVES, 4, rows // 2, width // WAVES), BF16),
        pltpu.VMEM((2, 8, tokens, rows), BF16),
        pltpu.VMEM((2, tokens, width), BF16),
        pltpu.VMEM((2, tokens, width), BF16),
        pltpu.VMEM((width, width), BF16),
        pltpu.VMEM((2, 4, deep, rows), BF16),
        pltpu.VMEM((2, deep, rows), BF16),
        pltpu.VMEM((4, deep, rows), BF16),
        pltpu.VMEM((deep, rows), BF16),
        pltpu.VMEM((2, 4, rows, rows), BF16),
        pltpu.VMEM((4, rows, rows), BF16),
        pltpu.VMEM((2, rows // 2, rows), BF16),
        pltpu.VMEM((4, rows // 2, rows), BF16),
        pltpu.VMEM((rows, width), BF16),
        pltpu.VMEM((width, width), BF16),
        pltpu.SemaphoreType.DMA((16,)),
        pltpu.SemaphoreType.DMA((MESSAGES,)),
        pltpu.SemaphoreType.DMA((MESSAGES,)),
    ]
    gathered, in_cov, out_cov = pl.pallas_call(
        kernel,
        out_shape=(
            pltpu.VMEM((total, width), BF16),
            pltpu.VMEM((rows, width), F32),
            pltpu.VMEM((out_rows, width), F32),
        ),
        in_specs=[anywhere] * 5 + [vmem] * 2,
        out_specs=(vmem, vmem, vmem),
        scratch_shapes=scratch,
        compiler_params=pltpu.CompilerParams(
            collective_id=0, has_side_effects=True, vmem_limit_bytes=52 * 2**20
        ),
        cost_estimate=pl.CostEstimate(flops=2 * 10**10, bytes_accessed=4 * 10**7, transcendentals=0),
        name="precondition",
    )(
        inputs,
        out_grads,
        kernel_grad,
        basis_in,
        basis_out,
        eigen_in,
        eigen_out,
    )
    return pl.pallas_call(
        functools.partial(finish, tokens=16 * tokens),
        out_shape=(
            jax.ShapeDtypeStruct((total, width), BF16),
            jax.ShapeDtypeStruct((rows, width), F32),
            jax.ShapeDtypeStruct((out_rows, width), F32),
        ),
        in_specs=[vmem] * 5,
        out_specs=(anywhere, anywhere, anywhere),
        scratch_shapes=[pltpu.VMEM((rows, width), F32), pltpu.VMEM((out_rows, width), F32), pltpu.SemaphoreType.DMA((3,))],
        compiler_params=pltpu.CompilerParams(vmem_limit_bytes=40 * 2**20),
        name="finish",
    )(gathered, in_cov, out_cov, old_in_factor, old_out_factor)


def solution(mesh):
    in_specs = (
        P("dp", None),
        P("dp", None),
        P("dp", "owner"),
        P(("dp", "owner"), None),
        P("owner", None),
        P("dp"),
        P("owner"),
        P("dp", "owner"),
        P(("owner", "dp"), None),
    )
    out_specs = (P(None, "owner"), P("dp", "owner"), P(("owner", "dp"), None))
    return jax.shard_map(shards, mesh=mesh, in_specs=in_specs, out_specs=out_specs, check_vma=False)
```
